32 devices in a mesh: row: 8 (over z, x), col: 4 (over y, core).
Axes of the slice: x: 2, y: 2, z: 4, core: 2. Of those that a mesh axis runs over, the one named last changes fastest.
Arguments:
- recorded: float32 [2, 2, 4096, 4096], P(None, None, 'row', 'col'), may hold values from -1.1 to 1.1, as said below
Outputs:
- multiples: float32 [2, 2, 4096, 4096], P(None, None, 'row', 'col')
The draws below stay inside these ranges and needn't reach their ends.
Inputs may be any that keep to these rules, and one draw needn't show every extreme that they name: Every frequency slice is reciprocal: recorded[c, f, s, r] = recorded[c, f, r, s] for both parts c.
All inputs are finite; a program needn't handle non-finite values.
Results may differ from the reference program's by a relative error of at most 0.00011.
Values sent between devices are 32-bit elements; how exact they have to be, the bound alone decides.
No kernel may reach another device: no remote copies, remote signals or barrier semaphores. Data moves between devices by JAX's collectives and lax.ppermute only.
A program may use at most 192 MiB of HBM per device.

```python
import jax
import jax.numpy as jnp
from jax import lax

N = 4096
F = 2


def draw_recorded(key, part):
    key = jax.random.fold_in(key, 7)
    first = jax.random.fold_in(key, 0)
    raw = jax.random.truncated_normal(first, -4.0, 4.0, (2, F, N, N), jnp.float32)
    return ((raw + jnp.swapaxes(raw, 2, 3)) * 0.0742).astype(jnp.float32)


def setup_inputs(seed: int = 0) -> dict:
    splits = jax.random.split(jax.random.key(seed), 2)
    recorded = draw_recorded(jax.random.fold_in(splits[1], 71), 0)
    return dict(recorded=recorded)


def matmul(left, right):
    return jnp.dot(left, right, precision=lax.Precision.HIGHEST, preferred_element_type=jnp.float32)


def one_frequency(pair):
    real_in, imag_in = pair
    real_out = matmul(real_in, real_in) - matmul(imag_in, imag_in)
    imag_out = matmul(real_in, imag_in) + matmul(imag_in, real_in)
    return (-real_out, -imag_out)


def reference(recorded):
    real_out, imag_out = lax.map(one_frequency, (recorded[0], recorded[1]))
    return jnp.stack([real_out, imag_out])
```

```python
import functools

import jax
import jax.numpy as jnp
from jax import lax
from jax.experimental import pallas as pl
from jax.experimental.pallas import tpu as pltpu
from jax.sharding import PartitionSpec as P

AXES = ("row", "col")
CHUNKS = 4


def dot(left, right):
    return jnp.dot(left, right, precision=lax.Precision.HIGH, preferred_element_type=jnp.float32)


def multiply(left, right):
    rr, ii = dot(left[0], right[0]), dot(left[1], right[1])
    ss = dot(left[0] + left[1], right[0] + right[1])
    return jnp.stack([rr - ii, ss - rr - ii])


def gathered(recorded):
    rows = lax.all_gather(recorded, "col", axis=3, tiled=True)
    columns = lax.all_gather(recorded, "row", axis=2, tiled=True)
    out = [multiply(rows[:, f], columns[:, f]) for f in range(recorded.shape[1])]
    return -jnp.stack(out, axis=1)


def split(value):
    high = value.astype(jnp.bfloat16)
    return high, (value - high.astype(jnp.float32)).astype(jnp.bfloat16)


def split_into(out, at, block, rows=slice(None)):
    k = block[0].shape[1]
    for c in range(3):
        v = block[c] if c < 2 else block[0] + block[1]
        out[2 * c, rows, at : at + k], out[2 * c + 1, rows, at : at + k] = split(v)


def split_kernel(*refs):
    at = 0
    for ref in refs[:-1]:
        split_into(refs[-1], at, ref)
        at += ref.shape[2]


def split_blocks(blocks):
    rows, ks = blocks[0].shape[1], [v.shape[2] for v in blocks]
    mb = rows // CHUNKS
    return pl.pallas_call(
        split_kernel,
        grid=(rows // mb,),
        in_specs=[pl.BlockSpec((2, mb, k), lambda i: (0, i, 0)) for k in ks],
        out_specs=pl.BlockSpec((6, mb, sum(ks)), lambda i: (0, i, 0)),
        out_shape=jax.ShapeDtypeStruct((6, rows, sum(ks)), jnp.bfloat16),
        compiler_params=pltpu.CompilerParams(vmem_limit_bytes=56 * 2**20),
        cost_estimate=pl.CostEstimate(flops=1000, bytes_accessed=1000, transcendentals=0),
    )(*blocks)


def product_kernel(role_ref, *refs, picks, lefts, rights, more, halves, fetch):
    left, candidates, rest = refs[:lefts], refs[lefts : lefts + rights], refs[lefts + rights :]
    base, rest = (rest[0], rest[1:]) if more else (None, rest)
    outs, rest = rest[:halves], rest[halves:]
    scratch = rest[0]
    j, i = pl.program_id(0), pl.program_id(1)
    for role, steps in picks.items():
        for step, pieces in enumerate(steps):

            @pl.when((role_ref[0] == role) & (i == 0) & (j == step))
            def _():
                if fetch:
                    staged, sems = rest[-2:]
                    at, copies = 0, []
                    for which, start, size, _, _, _ in pieces:
                        source = candidates[which].at[:, pl.ds(start, size), :]
                        copies.append(
                            pltpu.make_async_copy(source, staged.at[:, pl.ds(at, size), :], sems.at[len(copies)])
                        )
                        copies[-1].start()
                        at += size
                    at = 0
                for number, (which, start, size, flip, row, col) in enumerate(pieces):
                    if fetch:
                        copies[number].wait()
                        block = [staged[c, at : at + size, :] for c in range(2)]
                        at += size
                    else:
                        block = [candidates[which][c, start : start + size, :] for c in range(2)]
                    if flip:
                        block = [v.T for v in block]
                    split_into(scratch, col, block, slice(row, row + block[0].shape[0]))

    @pl.when(functools.reduce(jnp.logical_or, [role_ref[0] == role for role in picks]))
    def _():
        if lefts == 1:
            parts = multiply_split(left[0], slice(None), scratch)
        else:
            held = rest[1]
            mb = left[0].shape[1]
            rows = pl.ds(pl.multiple_of(i * mb, mb), mb)

            @pl.when(j == 0)
            def _():
                at = 0
                for ref in left:
                    split_into(held, at, ref, rows)
                    at += ref.shape[2]

            parts = multiply_split(held, rows, scratch)
        for h, out in enumerate(outs):

            @pl.when(i * halves // pl.num_programs(1) == h)
            def _():
                for c in range(2):
                    out[c] = parts[c] if base is None else parts[c] + base[c]


def multiply_split(left, rows, right):
    parts = []
    for c in range(3):
        high, low = left[2 * c, rows, :], left[2 * c + 1, rows, :]
        total = jnp.dot(high, right[2 * c], preferred_element_type=jnp.float32)
        total += jnp.dot(high, right[2 * c + 1], preferred_element_type=jnp.float32)
        total += jnp.dot(low, right[2 * c], preferred_element_type=jnp.float32)
        parts.append(total)
    rr, ii, ss = parts
    return rr - ii, ss - rr - ii


def product(role, left, rights, picks, columns, base=None, half=None, halves=1, fetch=False):
    split_left = not isinstance(left, list)
    lefts = [left] if split_left else left
    rows = lefts[0].shape[1]
    depth = sum(v.shape[2] for v in lefts) // (1 if half is None else 2)
    mb, nb = rows // CHUNKS, min(columns, rows // 2)
    once = pl.Buffered(1)

    def on(r):
        return functools.reduce(jnp.maximum, [jnp.where(r[0] == role_, 1, 0) for role_ in picks])

    if split_left:
        in_specs = [pl.BlockSpec((6, mb, depth), lambda j, i, r: (0, i * on(r), half or 0))]
    else:
        last = rows // mb - 1
        in_specs = [
            pl.BlockSpec((2, mb, v.shape[2]), lambda j, i, r: (0, jnp.where(j == 0, i, last) * on(r), 0)) for v in lefts
        ]
    arrays = []
    for v in rights:
        if fetch:
            arrays.append(v)
            spec = pl.BlockSpec(memory_space=pl.ANY)
        elif isinstance(v, tuple):
            arrays.append(v[0])
            spec = pl.BlockSpec((2, nb, v[0].shape[2]), lambda j, i, r: (0, j * on(r), 0), pipeline_mode=once)
        else:
            arrays.append(v)
            spec = pl.BlockSpec(v.shape, lambda j, i, r: (0, 0, 0), pipeline_mode=once)
        in_specs.append(spec)
    args = lefts + arrays
    if base is not None:
        in_specs.append(pl.BlockSpec((2, mb, nb), lambda j, i, r: (0, i * on(r), j * on(r))))
        args.append(base)
    scratch = [pltpu.VMEM((6, depth, nb), jnp.bfloat16)]
    if not split_left:
        scratch.append(pltpu.VMEM((6, rows, depth), jnp.bfloat16))
    if fetch:
        every = [pieces for steps in picks.values() for pieces in steps]
        scratch.append(pltpu.VMEM((2, max(sum(e[2] for e in v) for v in every), nb), jnp.float32))
        scratch.append(pltpu.SemaphoreType.DMA((max(len(v) for v in every),)))
    body = functools.partial(
        product_kernel, picks=picks, lefts=len(lefts), rights=len(rights), more=base is not None, halves=halves, fetch=fetch
    )
    steps = rows // mb // halves
    out_specs = [
        pl.BlockSpec((2, mb, nb), lambda j, i, r, h=h: (0, jnp.clip(i - h * steps, 0, steps - 1) * on(r), j * on(r)))
        for h in range(halves)
    ]
    out_shape = [jax.ShapeDtypeStruct((2, rows // halves, columns), jnp.float32)] * halves
    result = pl.pallas_call(
        body,
        grid_spec=pltpu.PrefetchScalarGridSpec(
            num_scalar_prefetch=1,
            grid=(columns // nb, rows // mb),
            in_specs=in_specs,
            out_specs=out_specs,
            scratch_shapes=scratch,
        ),
        out_shape=out_shape,
        compiler_params=pltpu.CompilerParams(vmem_limit_bytes=58 * 2**20),
        cost_estimate=pl.CostEstimate(flops=1000, bytes_accessed=1000, transcendentals=0),
    )(role, *args)
    return result[0] if halves == 1 else tuple(result)


def place_kernel(role_ref, *refs):
    (totals, gots, tops, crossed), out = (refs[:2], refs[2:4], refs[4:8], refs[8:12]), refs[12]
    f, j = pl.program_id(0), pl.program_id(1)
    kept = role_ref[1] == f
    for sources, flag in ((totals, kept), (gots, jnp.logical_not(kept))):
        for role, ref in enumerate(sources):

            @pl.when(flag & (role_ref[0] == role))
            def _():
                out[:, 0] = -ref[...]

    for sources, flag in ((tops, kept), (crossed, jnp.logical_not(kept))):
        for step, ref in enumerate(sources):

            @pl.when(flag & (role_ref[0] >= 2) & (j == step))
            def _():
                out[:, 0] = -ref[...]


def place(role, totals, gots, tops, crossed):
    _, rows, columns = totals[0].shape
    w = columns // CHUNKS
    in_specs = [
        pl.BlockSpec((2, rows, w), lambda f, j, r, k=k: (0, 0, j * jnp.where(r[0] == k, 1, 0))) for k in (0, 1, 0, 1)
    ] + [pl.BlockSpec((2, rows, w), lambda f, j, r: (0, 0, 0))] * 8
    return pl.pallas_call(
        place_kernel,
        grid_spec=pltpu.PrefetchScalarGridSpec(
            num_scalar_prefetch=1,
            grid=(2, CHUNKS),
            in_specs=in_specs,
            out_specs=pl.BlockSpec((2, 1, rows, w), lambda f, j, r: (0, f, 0, (j + 2 * f) % CHUNKS)),
        ),
        out_shape=jax.ShapeDtypeStruct((2, 2, rows, columns), jnp.float32),
        compiler_params=pltpu.CompilerParams(vmem_limit_bytes=56 * 2**20),
        cost_estimate=pl.CostEstimate(flops=1000, bytes_accessed=1000, transcendentals=0),
    )(role, *totals, *gots, *tops, *crossed)


def blocked(recorded):
    row, col = lax.axis_index("row"), lax.axis_index("col")
    z, x, y, c = row // 2, row % 2, col // 2, col % 2
    half, p = z // 2, z % 2
    diag, first, lane = y == half, c == p, c == half
    at_end = (z == 0) | (z == 3)
    role = jnp.where(diag, jnp.where(first, 0, 1), jnp.where(lane, 3, 2)).astype(jnp.int32)
    roles = jnp.reshape(role, (1,))
    part, width = recorded.shape[2], recorded.shape[3]
    w, n = width // CHUNKS, width

    def send(value, *moves):
        pairs = []
        for zz in range(4):
            for xx in range(2):
                for yy in range(2):
                    for cc in range(2):
                        for move in moves:
                            to = move(zz, xx, yy, cc)
                            if to is not None:
                                a, b, d, e = to
                                pairs.append((((zz * 2 + xx) * 2 + yy) * 2 + cc, ((a * 2 + b) * 2 + d) * 2 + e))
        return lax.ppermute(value, AXES, pairs)

    def on_diag(zz, yy):
        return yy == zz // 2

    swap_x = lambda a, b, d, e: (a, 1 - b, d, e)
    swap_y = lambda a, b, d, e: (a, b, 1 - d, e)
    swap_core = lambda a, b, d, e: (a, b, d, 1 - e)
    swap_core_diag = lambda a, b, d, e: (a, b, d, 1 - e) if on_diag(a, d) else None
    to_diag = lambda a, b, d, e: None if on_diag(a, d) else (a, b, 1 - d, e)
    to_off = lambda a, b, d, e: (a, b, 1 - d, e) if on_diag(a, d) else None
    swap_slab = lambda a, b, d, e: (a ^ 1, b, d, e) if on_diag(a, d) else None
    first_to_slab = lambda a, b, d, e: (a ^ 1, b, d, e) if on_diag(a, d) and e == a % 2 else None
    over_middle = lambda a, b, d, e: (3 - a, b, d, e) if on_diag(a, d) and a in (1, 2) else None
    middle_second = lambda a, b, d, e: (3 - a, b, d, e) if on_diag(a, d) and a in (1, 2) and e != a % 2 else None
    outward = lambda a, b, d, e: {1: (0, b, d, e), 2: (3, b, d, e)}.get(a) if not on_diag(a, d) else None
    outward_second = lambda a, b, d, e: outward(a, b, d, e) if e != a // 2 else None
    x_first = lambda a, b, d, e: (a, 1 - b, d, e) if on_diag(a, d) and e == a % 2 else None
    x_second = lambda a, b, d, e: (a, 1 - b, d, e) if on_diag(a, d) and e != a % 2 else None
    x_off = lambda a, b, d, e: None if on_diag(a, d) else (a, 1 - b, d, e)

    pick = jnp.where
    sync = lambda *values: lax.optimization_barrier(values)
    mid_off = jnp.logical_not(diag | at_end)

    def cut(f, j):
        start = (j * w + f * part) % width
        return lax.dynamic_slice(recorded, (0, f, 0, start), (2, 1, part, 2 * w))[:, 0]

    def chunk(value, j):
        return value[:, :, j * w : (j + 1) * w]

    mine, give = [cut(x, 0), cut(x, 2)], [cut(1 - x, 0), cut(1 - x, 2)]
    got = send(give[0], swap_x)
    own01 = jnp.concatenate([mine[0], got], 1)
    own = [chunk(own01, 0), chunk(own01, 1)]
    lows = jnp.concatenate([own[0], own[1][:, w:]], 1)
    own01, own[0], own[1], lows, give[1] = sync(own01, own[0], own[1], lows, give[1])

    right, there, seen, cores, seen_cores = [None] * 4, [None] * 4, [None] * 4, [None] * 4, [None] * 4
    got = send(give[1], swap_x)
    right[0] = send(own[0], to_diag, over_middle)
    low01 = send(lows, first_to_slab)
    core01 = send(own01, swap_core)
    own23 = jnp.concatenate([mine[1], got], 1)
    own += [chunk(own23, 0), chunk(own23, 1)]
    lows23 = jnp.concatenate([own[2][:, 2 * w :], own[3][:, 3 * w :]], 1)
    mixed = pick(diag & first, jnp.concatenate([own[1][:, w:], own[3][:, 3 * w :]], 1), own[1])
    own23, own[2], own[3], lows23, mixed, right[0], low01, core01 = sync(
        own23, own[2], own[3], lows23, mixed, right[0], low01, core01
    )
    core23 = send(own23, swap_core)
    core23, own[3], lows23, mixed, right[0] = sync(core23, own[3], lows23, mixed, right[0])

    def whole(which, k, row, transposed=False):
        return (which, 0, k, transposed, row, 0)

    def lower(sources, j, row, col):
        out = [(sources[i][0], sources[i][1] + (j - i) * w, w, True, row + i * w, col) for i in range(j)]
        return out + [(sources[j][0], sources[j][1], n - j * w, False, row + j * w, col)]

    there[0] = send(right[0], swap_slab, outward)
    right[1] = send(mixed, to_diag, over_middle)
    low23 = send(lows23, first_to_slab)
    cores[0] = send(right[0], swap_core_diag)
    left = split_blocks([own01, own23, core01, core23])
    both = [[whole(0, n // 2, 0, True), whole(1, n // 2, n // 2, True)]] * 2
    total = product(
        roles,
        left,
        [(core01, "rows"), (core23, "rows"), own01, own23],
        {0: both, 1: [[whole(2, n, 0)], [whole(3, n, 0)]]},
        n,
        half=1,
    )
    mixed = pick(diag & first, chunk(core23, 1), own[2])
    seen[0] = pick(mid_off, right[0], there[0])
    there[0], right[1], low01, low23, cores[0], left, total, mixed, seen[0] = sync(
        there[0], right[1], low01, low23, cores[0], left, total, mixed, seen[0]
    )

    def share(j):
        r, t = right[j], there[j]
        return product(
            roles, left, [r, t], {0: [[whole(0, n, 0), whole(1, n, n)]], 1: [[whole(1, n, 0), whole(0, n, n)]]}, w, fetch=True
        )

    def add_rights(total, j, role_, halves=1):
        these = [right[j], right[j + 1], cores[j], cores[j + 1]]
        others = [there[j], there[j + 1], seen_cores[j], seen_cores[j + 1]] if role_ else these
        pieces = [whole(i, n // 2, i * w, True) for i in range(4)]
        return product(roles, these, [(v, "rows") for v in others], {role_: [pieces, pieces]}, n, base=total, halves=halves)

    shares, shared = [None] * 4, [None] * 4
    there[1] = send(right[1], swap_slab, outward)
    right[2] = send(mixed, to_diag, over_middle)
    cores[1] = send(right[1], swap_core_diag)
    seen_cores[0] = send(seen[0], swap_core)
    shares[0] = share(0)
    low_sources = [(2, 0), (2, n), (3, 0), (3, 2 * w)]
    total = product(
        roles,
        left,
        [(own01, "rows"), (own23, "rows"), low01, low23],
        {
            0: both,
            1: [lower(low_sources, 2 * j, 0, 0) + lower(low_sources, 2 * j + 1, 0, w) for j in range(2)],
        },
        n,
        base=total,
        half=0,
    )
    mixed = pick(diag, shares[0], own[3])
    seen[1] = pick(mid_off, right[1], there[1])
    there[1], right[2], low01, low23, cores[1], seen_cores[0], total, mixed, seen[1] = sync(
        there[1], right[2], low01, low23, cores[1], seen_cores[0], total, mixed, seen[1]
    )

    there[2] = send(right[2], swap_slab, outward)
    right[3] = send(mixed, swap_y)
    near3 = send(low01, middle_second)
    cores[2] = send(right[2], swap_core_diag)
    seen_cores[1] = send(seen[1], swap_core)
    shares[1] = share(1)
    total_first = add_rights(total, 0, 0)
    seen[2] = pick(mid_off, right[2], there[2])
    mixed = pick(diag & first, lows23, low23)
    swapped = pick(diag, right[3], seen[2])
    there[2], right[3], near3, cores[2], seen_cores[1], shares[1], total_first, swapped, mixed = sync(
        there[2], right[3], near3, cores[2], seen_cores[1], shares[1], total_first, swapped, mixed
    )
    shared[0] = right[3]

    there[3] = send(right[3], swap_slab)
    shared[1] = send(shares[1], to_off)
    near4 = send(mixed, over_middle)
    far3 = send(near3, outward_second)
    swapped = send(swapped, swap_core)
    shares[2] = share(2)
    shares[2], total_first, swapped = sync(shares[2], total_first, swapped)
    cores[3] = swapped
    keep_first, to_first = add_rights(total_first, 2, 0, 2)
    to_first, total = sync(to_first, total)
    total_second = add_rights(total, 0, 1)
    far3 = pick(at_end, far3, near3)
    there[3], shared[1], near4, far3, swapped, shares[2], keep_first, to_first, total_second = sync(
        there[3], shared[1], near4, far3, swapped, shares[2], keep_first, to_first, total_second
    )

    def rest(j, base):
        rights = seen[:3] + seen_cores[:2] + [swapped, far3, far4]
        lane_low = [(0, 0), (1, 0), (7, 0), (1, 3 * w)]
        other_low = [(6, 0), (6, n), (7, 0), (7, 2 * w)]
        picks = {
            2: lower(other_low, j, 0, 0) + [whole((0, 1, 2, 5)[j], n, n)],
            3: lower(lane_low, j, 0, 0) + [(v, j * w, w, True, n + k * w, 0) for k, v in enumerate((3, 4, 5, 2))],
        }
        used = sorted({entry[0] for pieces in picks.values() for entry in pieces})
        picks = {r: [[(used.index(e[0]),) + e[1:] for e in v]] for r, v in picks.items()}
        return product(roles, left, [rights[i] for i in used], picks, w, base=base, halves=2, fetch=True)

    tops, downs, crossed = [None] * 4, [None] * 4, [None] * 4
    shared[2] = send(shares[2], to_off)
    far4 = send(near4, outward)
    seen_cores[2] = send(there[2], swap_core_diag)
    seen_cores[3] = send(there[3], swap_core_diag)
    got_first = send(to_first, x_first)
    shares[3] = share(3)
    shares[3], shared[0], seen_cores[2], seen_cores[3] = sync(shares[3], shared[0], seen_cores[2], seen_cores[3])
    shared[3] = send(shares[3], to_off)
    tops[0], downs[0] = rest(0, shared[0])
    downs[0], shared[1] = sync(downs[0], shared[1])
    crossed[0] = send(downs[0], x_off)
    tops[1], downs[1] = rest(1, shared[1])
    downs[1], total_second = sync(downs[1], total_second)
    crossed[1] = send(downs[1], x_off)
    keep_second, to_second = add_rights(total_second, 2, 1, 2)
    far4 = pick(at_end, far4, near4)
    to_second, shared[2], far4, crossed[0] = sync(to_second, shared[2], far4, crossed[0])
    got_second = send(to_second, x_second)
    tops[2], downs[2] = rest(2, shared[2])
    downs[2], shared[3], crossed[1], got_first = sync(downs[2], shared[3], crossed[1], got_first)
    crossed[2] = send(downs[2], x_off)
    tops[3], downs[3] = rest(3, shared[3])
    downs[3], crossed[2] = sync(downs[3], crossed[2])
    crossed[3] = send(downs[3], x_off)

    flags = jnp.stack([role, x.astype(jnp.int32)])
    return place(flags, [keep_first, keep_second], [got_first, got_second], tops, crossed)


def solution(mesh):
    rows, cols = mesh.shape["row"], mesh.shape["col"]

    def body(recorded):
        frequencies = recorded.shape[1]
        if frequencies == 2 and cols == 4 and rows == frequencies * cols:
            return blocked(recorded)
        return gathered(recorded)

    spec = P(None, None, "row", "col")
    return jax.shard_map(body, mesh=mesh, in_specs=(spec,), out_specs=spec, check_vma=False)
```

```python
import functools

import jax
import jax.numpy as jnp
from jax import lax
from jax.experimental import pallas as pl
from jax.experimental.pallas import tpu as pltpu
from jax.sharding import PartitionSpec as P

AXES = ("row", "col")
CHUNKS = 4


def dot(left, right):
    return jnp.dot(left, right, precision=lax.Precision.HIGH, preferred_element_type=jnp.float32)


def multiply(left, right):
    rr, ii = dot(left[0], right[0]), dot(left[1], right[1])
    ss = dot(left[0] + left[1], right[0] + right[1])
    return jnp.stack([rr - ii, ss - rr - ii])


def gathered(recorded):
    rows = lax.all_gather(recorded, "col", axis=3, tiled=True)
    columns = lax.all_gather(recorded, "row", axis=2, tiled=True)
    out = [multiply(rows[:, f], columns[:, f]) for f in range(recorded.shape[1])]
    return -jnp.stack(out, axis=1)


def split(value):
    high = value.astype(jnp.bfloat16)
    return high, (value - high.astype(jnp.float32)).astype(jnp.bfloat16)


def split_into(out, at, block, rows=slice(None)):
    k = block[0].shape[1]
    for c in range(3):
        v = block[c] if c < 2 else block[0] + block[1]
        out[2 * c, rows, at : at + k], out[2 * c + 1, rows, at : at + k] = split(v)


def product_kernel(role_ref, *refs, picks, lefts, rights, more, halves, fetch, depth, keep):
    left, candidates, rest = refs[:lefts], refs[lefts : lefts + rights], refs[lefts + rights :]
    base, rest = (rest[0], rest[1:]) if more else (None, rest)
    outs, rest = rest[:halves], rest[halves:]
    kept, rest = (rest[0], rest[1:]) if keep else (None, rest)
    scratch = rest[0]
    j, i = pl.program_id(0), pl.program_id(1)
    for role, steps in picks.items():
        for step, pieces in enumerate(steps):

            @pl.when((role_ref[0] == role) & (i == 0) & (j == step))
            def _():
                if fetch:
                    staged, sems = rest[-2:]
                    at, copies = 0, []
                    for which, start, size, _, _, _ in pieces:
                        source = candidates[which].at[:, pl.ds(start, size), :]
                        k = source.shape[2]
                        target = staged.at[:, pl.ds(at, size), pl.ds(0, k)]
                        copies.append(pltpu.make_async_copy(source, target, sems.at[len(copies)]))
                        copies[-1].start()
                        at += size
                    at = 0
                for number, (which, start, size, flip, row, col) in enumerate(pieces):
                    if fetch:
                        copies[number].wait()
                        k = candidates[which].shape[2]
                        block = [staged[c, at : at + size, :k] for c in range(2)]
                        at += size
                    else:
                        block = [candidates[which][c, start : start + size, :] for c in range(2)]
                    if flip:
                        block = [v.T for v in block]
                    split_into(scratch, col, block, slice(row, row + block[0].shape[0]))

    def split_left(held):
        at = 0
        for ref in left:
            split_into(held, at, ref)
            at += ref.shape[2]

    if keep:
        split_left(kept)

    @pl.when(functools.reduce(jnp.logical_or, [role_ref[0] == role for role in picks]))
    def _():
        if keep:
            parts = multiply_split(kept, slice(kept.shape[2] - depth, None), scratch)
        elif lefts == 1:
            parts = multiply_split(left[0], slice(None), scratch)
        else:
            split_left(rest[1])
            parts = multiply_split(rest[1], slice(None), scratch)
        for h, out in enumerate(outs):

            @pl.when(i * halves // pl.num_programs(1) == h)
            def _():
                for c in range(2):
                    out[c] = parts[c] if base is None else parts[c] + base[c]


def multiply_split(left, columns, right):
    parts = []
    for c in range(3):
        high, low = left[2 * c, :, columns], left[2 * c + 1, :, columns]
        total = jnp.dot(high, right[2 * c], preferred_element_type=jnp.float32)
        total += jnp.dot(high, right[2 * c + 1], preferred_element_type=jnp.float32)
        total += jnp.dot(low, right[2 * c], preferred_element_type=jnp.float32)
        parts.append(total)
    rr, ii, ss = parts
    return rr - ii, ss - rr - ii


def product(role, left, rights, picks, columns, base=None, half=None, halves=1, fetch=False, keep=False):
    split_left = not isinstance(left, list)
    lefts = [left] if split_left else left
    rows = lefts[0].shape[1]
    total = sum(v.shape[2] for v in lefts)
    depth = total // (1 if half is None and not keep else 2)
    mb, nb = rows // CHUNKS, columns
    once = pl.Buffered(1)

    def on(r):
        return functools.reduce(jnp.maximum, [jnp.where(r[0] == role_, 1, 0) for role_ in picks])

    if split_left:
        in_specs = [pl.BlockSpec((6, mb, depth), lambda j, i, r: (0, i * on(r), half or 0))]
    else:
        in_specs = [
            pl.BlockSpec((2, mb, v.shape[2]), lambda j, i, r: (0, i * (1 if keep else on(r)), 0)) for v in lefts
        ]
    arrays = []
    for v in rights:
        if fetch:
            arrays.append(v)
            spec = pl.BlockSpec(memory_space=pl.ANY)
        elif isinstance(v, tuple):
            arrays.append(v[0])
            spec = pl.BlockSpec((2, nb, v[0].shape[2]), lambda j, i, r: (0, j * on(r), 0), pipeline_mode=once)
        else:
            arrays.append(v)
            spec = pl.BlockSpec(v.shape, lambda j, i, r: (0, 0, 0), pipeline_mode=once)
        in_specs.append(spec)
    args = lefts + arrays
    if base is not None:
        in_specs.append(pl.BlockSpec((2, mb, nb), lambda j, i, r: (0, i * on(r), j * on(r))))
        args.append(base)
    scratch = [pltpu.VMEM((6, depth, nb), jnp.bfloat16)]
    if not split_left and not keep:
        scratch.append(pltpu.VMEM((6, mb, depth), jnp.bfloat16))
    if fetch:
        every = [pieces for steps in picks.values() for pieces in steps]
        wide = max(v.shape[2] for v in rights)
        scratch.append(pltpu.VMEM((2, max(sum(e[2] for e in v) for v in every), wide), jnp.float32))
        scratch.append(pltpu.SemaphoreType.DMA((max(len(v) for v in every),)))
    body = functools.partial(
        product_kernel, picks=picks, lefts=len(lefts), rights=len(rights), more=base is not None, halves=halves, fetch=fetch,
        depth=depth, keep=keep,
    )
    steps = rows // mb // halves
    out_specs = [
        pl.BlockSpec((2, mb, nb), lambda j, i, r, h=h: (0, jnp.clip(i - h * steps, 0, steps - 1) * on(r), j * on(r)))
        for h in range(halves)
    ]
    out_shape = [jax.ShapeDtypeStruct((2, rows // halves, columns), jnp.float32)] * halves
    if keep:
        out_specs.append(pl.BlockSpec((6, mb, total), lambda j, i, r: (0, i, 0)))
        out_shape.append(jax.ShapeDtypeStruct((6, rows, total), jnp.bfloat16))
    result = pl.pallas_call(
        body,
        grid_spec=pltpu.PrefetchScalarGridSpec(
            num_scalar_prefetch=1,
            grid=(columns // nb, rows // mb),
            in_specs=in_specs,
            out_specs=out_specs,
            scratch_shapes=scratch,
        ),
        out_shape=out_shape,
        compiler_params=pltpu.CompilerParams(vmem_limit_bytes=58 * 2**20),
        cost_estimate=pl.CostEstimate(flops=1000, bytes_accessed=1000, transcendentals=0),
    )(role, *args)
    return tuple(result) if len(result) > 1 else result[0]


def place_kernel(role_ref, *refs):
    (totals, gots, tops, crossed), out = (refs[:2], refs[2:4], refs[4:8], refs[8:12]), refs[12]
    f, j = pl.program_id(0), pl.program_id(1)
    kept = role_ref[1] == f
    for sources, flag in ((totals, kept), (gots, jnp.logical_not(kept))):
        for role, ref in enumerate(sources):

            @pl.when(flag & (role_ref[0] == role))
            def _():
                out[:, 0] = -ref[...]

    for sources, flag in ((tops, kept), (crossed, jnp.logical_not(kept))):
        for step, ref in enumerate(sources):

            @pl.when(flag & (role_ref[0] >= 2) & (j == step))
            def _():
                out[:, 0] = -ref[...]


def place(role, totals, gots, tops, crossed):
    _, rows, columns = totals[0].shape
    w = columns // CHUNKS
    in_specs = [
        pl.BlockSpec((2, rows, w), lambda f, j, r, k=k: (0, 0, j * jnp.where(r[0] == k, 1, 0))) for k in (0, 1, 0, 1)
    ] + [pl.BlockSpec((2, rows, w), lambda f, j, r: (0, 0, 0))] * 8
    return pl.pallas_call(
        place_kernel,
        grid_spec=pltpu.PrefetchScalarGridSpec(
            num_scalar_prefetch=1,
            grid=(2, CHUNKS),
            in_specs=in_specs,
            out_specs=pl.BlockSpec((2, 1, rows, w), lambda f, j, r: (0, f, 0, (j + 2 * f) % CHUNKS)),
        ),
        out_shape=jax.ShapeDtypeStruct((2, 2, rows, columns), jnp.float32),
        compiler_params=pltpu.CompilerParams(vmem_limit_bytes=56 * 2**20),
        cost_estimate=pl.CostEstimate(flops=1000, bytes_accessed=1000, transcendentals=0),
    )(role, *totals, *gots, *tops, *crossed)


def blocked(recorded):
    row, col = lax.axis_index("row"), lax.axis_index("col")
    z, x, y, c = row // 2, row % 2, col // 2, col % 2
    half, p = z // 2, z % 2
    diag, first, lane = y == half, c == p, c == half
    at_end = (z == 0) | (z == 3)
    role = jnp.where(diag, jnp.where(first, 0, 1), jnp.where(lane, 3, 2) + jnp.where(at_end, 0, 2)).astype(jnp.int32)
    roles = jnp.reshape(role, (1,))
    part, width = recorded.shape[2], recorded.shape[3]
    w, n = width // CHUNKS, width

    def send(value, *moves):
        pairs = []
        for zz in range(4):
            for xx in range(2):
                for yy in range(2):
                    for cc in range(2):
                        for move in moves:
                            to = move(zz, xx, yy, cc)
                            if to is not None:
                                a, b, d, e = to
                                pairs.append((((zz * 2 + xx) * 2 + yy) * 2 + cc, ((a * 2 + b) * 2 + d) * 2 + e))
        return lax.ppermute(value, AXES, pairs)

    def on_diag(zz, yy):
        return yy == zz // 2

    swap_x = lambda a, b, d, e: (a, 1 - b, d, e)
    swap_y = lambda a, b, d, e: (a, b, 1 - d, e)
    swap_core = lambda a, b, d, e: (a, b, d, 1 - e)
    swap_core_diag = lambda a, b, d, e: (a, b, d, 1 - e) if on_diag(a, d) else None
    to_diag = lambda a, b, d, e: None if on_diag(a, d) else (a, b, 1 - d, e)
    to_off = lambda a, b, d, e: (a, b, 1 - d, e) if on_diag(a, d) else None
    swap_slab = lambda a, b, d, e: (a ^ 1, b, d, e) if on_diag(a, d) else None
    first_to_slab = lambda a, b, d, e: (a ^ 1, b, d, e) if on_diag(a, d) and e == a % 2 else None
    over_middle = lambda a, b, d, e: (3 - a, b, d, e) if on_diag(a, d) and a in (1, 2) else None
    middle_second = lambda a, b, d, e: (3 - a, b, d, e) if on_diag(a, d) and a in (1, 2) and e != a % 2 else None
    outward = lambda a, b, d, e: {1: (0, b, d, e), 2: (3, b, d, e)}.get(a) if not on_diag(a, d) else None
    outward_second = lambda a, b, d, e: outward(a, b, d, e) if e != a // 2 else None
    x_first = lambda a, b, d, e: (a, 1 - b, d, e) if on_diag(a, d) and e == a % 2 else None
    x_second = lambda a, b, d, e: (a, 1 - b, d, e) if on_diag(a, d) and e != a % 2 else None
    x_off = lambda a, b, d, e: None if on_diag(a, d) else (a, 1 - b, d, e)

    pick = jnp.where
    sync = lambda *values: lax.optimization_barrier(values)
    mid_off = jnp.logical_not(diag | at_end)

    def cut(f, j):
        start = (j * w + f * part) % width
        return lax.dynamic_slice(recorded, (0, f, 0, start), (2, 1, part, 2 * w))[:, 0]

    def chunk(value, j):
        return value[:, :, j * w : (j + 1) * w]

    mine, give = [cut(x, 0), cut(x, 2)], [cut(1 - x, 0), cut(1 - x, 2)]
    got = send(give[0], swap_x)
    own01 = jnp.concatenate([mine[0], got], 1)
    own = [chunk(own01, 0), chunk(own01, 1)]
    lows = jnp.concatenate([own[0], own[1][:, w:]], 1)
    own01, own[0], own[1], lows, give[1] = sync(own01, own[0], own[1], lows, give[1])

    right, there, seen, cores, seen_cores = [None] * 4, [None] * 4, [None] * 4, [None] * 4, [None] * 4
    got = send(give[1], swap_x)
    right[0] = send(own[0], to_diag, over_middle)
    low01 = send(lows, first_to_slab)
    core01 = send(own01, swap_core)
    own23 = jnp.concatenate([mine[1], got], 1)
    own += [chunk(own23, 0), chunk(own23, 1)]
    lows23 = jnp.concatenate([own[2][:, 2 * w :], own[3][:, 3 * w :]], 1)
    mixed = pick(diag & first, jnp.concatenate([own[1][:, w:], own[3][:, 3 * w :]], 1), own[1])
    own23, own[2], own[3], lows23, mixed, right[0], low01, core01 = sync(
        own23, own[2], own[3], lows23, mixed, right[0], low01, core01
    )
    core23 = send(own23, swap_core)

    def whole(which, k, row, transposed=False):
        return (which, 0, k, transposed, row, 0)

    def lower(sources, j, row, col):
        out = [(sources[i][0], sources[i][1] + (j - i) * w, w, True, row + i * w, col) for i in range(j)]
        return out + [(sources[j][0], sources[j][1], n - j * w, False, row + j * w, col)]

    there[0] = send(right[0], swap_slab, outward)
    right[1] = send(mixed, to_diag, over_middle)
    low23 = send(lows23, first_to_slab)
    cores[0] = send(right[0], swap_core_diag)
    both = [whole(0, n, 0, True), whole(1, n, n // 2, True)]
    total, left = product(
        roles,
        [own01, own23, core01, core23],
        [core01, core23, own01, own23],
        {0: [both], 1: [[whole(2, n, 0), (3, 0, n, False, 0, n // 2)]]},
        n,
        fetch=True,
        keep=True,
    )
    there[0], right[1], total, left = sync(there[0], right[1], total, left)
    mixed = pick(diag & first, chunk(core23, 1), own[2])
    seen[0] = pick(mid_off, right[0], there[0])
    there[0], right[1], low01, low23, cores[0], left, total, mixed, seen[0], own[3] = sync(
        there[0], right[1], low01, low23, cores[0], left, total, mixed, seen[0], own[3]
    )

    def share(j):
        r, t = right[j], there[j]
        return product(
            roles, left, [r, t], {0: [[whole(0, n, 0), whole(1, n, n)]], 1: [[whole(1, n, 0), whole(0, n, n)]]}, w, fetch=True
        )

    def add_rights(total, js, active, halves=1):
        these = [right[j] for j in js] + [cores[j] for j in js]
        others = [there[j] for j in js] + [seen_cores[j] for j in js]
        k = len(these)
        rights = (these if 0 in active else []) + (others if 1 in active else [])
        first_of = {0: 0, 1: len(rights) - k}
        picks = {v: [[whole(first_of[v] + i, n, i * w, True) for i in range(k)]] for v in active}
        return product(roles, these, rights, picks, n, base=total, halves=halves, fetch=True)

    shares, shared = [None] * 4, [None] * 4
    there[1] = send(right[1], swap_slab, outward)
    right[2] = send(mixed, to_diag, over_middle)
    cores[1] = send(right[1], swap_core_diag)
    seen_cores[0] = send(seen[0], swap_core)
    shares[0] = share(0)
    low_sources = [(2, 0), (2, n), (3, 0), (3, 2 * w)]
    total = product(
        roles,
        left,
        [own01, own23, low01, low23],
        {0: [both], 1: [sum([lower(low_sources, j, 0, j * w) for j in range(4)], [])]},
        n,
        base=total,
        half=0,
        fetch=True,
    )
    mixed = pick(diag, shares[0], own[3])
    seen[1] = pick(mid_off, right[1], there[1])
    there[1], right[2], low01, low23, cores[1], seen_cores[0], total, mixed, seen[1] = sync(
        there[1], right[2], low01, low23, cores[1], seen_cores[0], total, mixed, seen[1]
    )

    there[2] = send(right[2], swap_slab, outward)
    right[3] = send(mixed, swap_y)
    near3 = send(low01, middle_second)
    cores[2] = send(right[2], swap_core_diag)
    seen_cores[1] = send(seen[1], swap_core)
    shares[1] = share(1)
    shares[1], seen_cores[1], cores[1], total = sync(shares[1], seen_cores[1], cores[1], total)
    total = add_rights(total, (0, 1), (0, 1))
    seen[2] = pick(mid_off, right[2], there[2])
    mixed = pick(diag & first, lows23, low23)
    swapped = pick(diag, right[3], seen[2])
    there[2], right[3], near3, cores[2], shares[1], total, swapped, mixed = sync(
        there[2], right[3], near3, cores[2], shares[1], total, swapped, mixed
    )
    shared[0] = right[3]

    there[3] = send(right[3], swap_slab)
    shared[1] = send(shares[1], to_off)
    near4 = send(mixed, over_middle)
    far3 = send(near3, outward_second)
    swapped = send(swapped, swap_core)
    shares[2] = share(2)
    shares[2], total, swapped = sync(shares[2], total, swapped)
    cores[3] = swapped
    keep_first, to_first = add_rights(total, (2, 3), (0,), 2)
    there[3], shared[1], near4, far3, swapped, shares[2], keep_first, to_first, total = sync(
        there[3], shared[1], near4, far3, swapped, shares[2], keep_first, to_first, total
    )

    def rest(j, base):
        rights = seen[:3] + seen_cores[:2] + [swapped, far3, far4, near3, near4]
        picks = {}
        for k, last in ((2, 6), (4, 8)):
            lane_low = [(0, 0), (1, 0), (last + 1, 0), (1, 3 * w)]
            other_low = [(last, 0), (last, n), (last + 1, 0), (last + 1, 2 * w)]
            picks[k] = lower(other_low, j, 0, 0) + [whole((0, 1, 2, 5)[j], n, n)]
            picks[k + 1] = lower(lane_low, j, 0, 0)
            picks[k + 1] += [(v, j * w, w, True, n + i * w, 0) for i, v in enumerate((3, 4, 5, 2))]
        used = sorted({entry[0] for pieces in picks.values() for entry in pieces})
        picks = {r: [[(used.index(e[0]),) + e[1:] for e in v]] for r, v in picks.items()}
        return product(roles, left, [rights[i] for i in used], picks, w, base=base, halves=2, fetch=True)

    tops, downs, crossed = [None] * 4, [None] * 4, [None] * 4
    shared[2] = send(shares[2], to_off)
    far4 = send(near4, outward)
    seen_cores[2] = send(there[2], swap_core_diag)
    seen_cores[3] = send(there[3], swap_core_diag)
    got_first = send(to_first, x_first)
    shares[3] = share(3)
    shares[3], shared[0], seen_cores[2], seen_cores[3] = sync(shares[3], shared[0], seen_cores[2], seen_cores[3])
    shared[3] = send(shares[3], to_off)
    tops[0], downs[0] = rest(0, shared[0])
    downs[0], shared[1] = sync(downs[0], shared[1])
    crossed[0] = send(downs[0], x_off)
    tops[1], downs[1] = rest(1, shared[1])
    downs[1], total = sync(downs[1], total)
    crossed[1] = send(downs[1], x_off)
    keep_second, to_second = add_rights(total, (2, 3), (1,), 2)
    to_second, shared[2], far4, crossed[0] = sync(to_second, shared[2], far4, crossed[0])
    got_second = send(to_second, x_second)
    tops[2], downs[2] = rest(2, shared[2])
    downs[2], shared[3], crossed[1], got_first = sync(downs[2], shared[3], crossed[1], got_first)
    crossed[2] = send(downs[2], x_off)
    tops[3], downs[3] = rest(3, shared[3])
    downs[3], crossed[2] = sync(downs[3], crossed[2])
    crossed[3] = send(downs[3], x_off)

    flags = jnp.stack([role, x.astype(jnp.int32)])
    return place(flags, [keep_first, keep_second], [got_first, got_second], tops, crossed)


def solution(mesh):
    rows, cols = mesh.shape["row"], mesh.shape["col"]

    def body(recorded):
        frequencies = recorded.shape[1]
        if frequencies == 2 and cols == 4 and rows == frequencies * cols:
            return blocked(recorded)
        return gathered(recorded)

    spec = P(None, None, "row", "col")
    return jax.shard_map(body, mesh=mesh, in_specs=(spec,), out_specs=spec, check_vma=False)
```

```python
import functools

import jax
import jax.numpy as jnp
from jax import lax
from jax.experimental import pallas as pl
from jax.experimental.pallas import tpu as pltpu
from jax.sharding import PartitionSpec as P

AXES = ("row", "col")
CHUNKS = 4


def dot(left, right):
    return jnp.dot(left, right, precision=lax.Precision.HIGH, preferred_element_type=jnp.float32)


def multiply(left, right):
    rr, ii = dot(left[0], right[0]), dot(left[1], right[1])
    ss = dot(left[0] + left[1], right[0] + right[1])
    return jnp.stack([rr - ii, ss - rr - ii])


def gathered(recorded):
    rows = lax.all_gather(recorded, "col", axis=3, tiled=True)
    columns = lax.all_gather(recorded, "row", axis=2, tiled=True)
    out = [multiply(rows[:, f], columns[:, f]) for f in range(recorded.shape[1])]
    return -jnp.stack(out, axis=1)


def split(value):
    high = value.astype(jnp.bfloat16)
    return high, (value - high.astype(jnp.float32)).astype(jnp.bfloat16)


def split_into(out, at, block, rows=slice(None)):
    k = block[0].shape[1]
    for c in range(3):
        v = block[c] if c < 2 else block[0] + block[1]
        out[2 * c, rows, at : at + k], out[2 * c + 1, rows, at : at + k] = split(v)


def product_kernel(role_ref, *refs, picks, lefts, rights, more, halves, fetch, depth, keep, negate):
    left, candidates, rest = refs[:lefts], refs[lefts : lefts + rights], refs[lefts + rights :]
    base, rest = (rest[0], rest[1:]) if more else (None, rest)
    outs, rest = rest[:halves], rest[halves:]
    kept, rest = (rest[0], rest[1:]) if keep else (None, rest)
    scratch = rest[0]
    j, i = pl.program_id(0), pl.program_id(1)
    for role, steps in picks.items():
        for step, pieces in enumerate(steps):

            @pl.when((role_ref[0] == role) & (i == 0) & (j == step))
            def _():
                if fetch:
                    staged, sems = rest[-2:]
                    at, copies = 0, []
                    for which, start, size, _, _, _ in pieces:
                        source = candidates[which].at[:, pl.ds(start, size), :]
                        k = source.shape[2]
                        target = staged.at[:, pl.ds(at, size), pl.ds(0, k)]
                        copies.append(pltpu.make_async_copy(source, target, sems.at[len(copies)]))
                        copies[-1].start()
                        at += size
                    at = 0
                for number, (which, start, size, flip, row, col) in enumerate(pieces):
                    if fetch:
                        copies[number].wait()
                        k = candidates[which].shape[2]
                        block = [staged[c, at : at + size, :k] for c in range(2)]
                        at += size
                    else:
                        block = [candidates[which][c, start : start + size, :] for c in range(2)]
                    if flip:
                        block = [v.T for v in block]
                    split_into(scratch, col, block, slice(row, row + block[0].shape[0]))

    def split_left(held):
        at = 0
        for ref in left:
            split_into(held, at, ref)
            at += ref.shape[2]

    if keep:
        split_left(kept)

    @pl.when(functools.reduce(jnp.logical_or, [role_ref[0] == role for role in picks]))
    def _():
        if keep:
            parts = multiply_split(kept, slice(kept.shape[2] - depth, None), scratch)
        elif lefts == 1:
            parts = multiply_split(left[0], slice(None), scratch)
        else:
            split_left(rest[1])
            parts = multiply_split(rest[1], slice(None), scratch)
        for h, out in enumerate(outs):

            @pl.when(i * min(halves, 2) // pl.num_programs(1) == min(h, 1))
            def _():
                for at, c in enumerate((h - 1,) if halves == 3 and h else (0, 1)):
                    value = parts[c] if base is None else parts[c] + base[c]
                    out[at] = -value if negate else value


def multiply_split(left, columns, right):
    parts = []
    for c in range(3):
        high, low = left[2 * c, :, columns], left[2 * c + 1, :, columns]
        total = jnp.dot(high, right[2 * c], preferred_element_type=jnp.float32)
        total += jnp.dot(high, right[2 * c + 1], preferred_element_type=jnp.float32)
        total += jnp.dot(low, right[2 * c], preferred_element_type=jnp.float32)
        parts.append(total)
    rr, ii, ss = parts
    return rr - ii, ss - rr - ii


def product(role, left, rights, picks, columns, base=None, half=None, halves=1, fetch=False, keep=False, negate=False):
    split_left = not isinstance(left, list)
    lefts = [left] if split_left else left
    rows = lefts[0].shape[1]
    total = sum(v.shape[2] for v in lefts)
    depth = total // (1 if half is None and not keep else 2)
    mb, nb = rows // CHUNKS, columns
    once = pl.Buffered(1)

    def on(r):
        return functools.reduce(jnp.maximum, [jnp.where(r[0] == role_, 1, 0) for role_ in picks])

    if split_left:
        in_specs = [pl.BlockSpec((6, mb, depth), lambda j, i, r: (0, i * on(r), half or 0))]
    else:
        in_specs = [
            pl.BlockSpec((2, mb, v.shape[2]), lambda j, i, r: (0, i * (1 if keep else on(r)), 0)) for v in lefts
        ]
    arrays = []
    for v in rights:
        if fetch:
            arrays.append(v)
            spec = pl.BlockSpec(memory_space=pl.ANY)
        elif isinstance(v, tuple):
            arrays.append(v[0])
            spec = pl.BlockSpec((2, nb, v[0].shape[2]), lambda j, i, r: (0, j * on(r), 0), pipeline_mode=once)
        else:
            arrays.append(v)
            spec = pl.BlockSpec(v.shape, lambda j, i, r: (0, 0, 0), pipeline_mode=once)
        in_specs.append(spec)
    args = lefts + arrays
    if base is not None:
        in_specs.append(pl.BlockSpec((2, mb, nb), lambda j, i, r: (0, i * on(r), j * on(r))))
        args.append(base)
    scratch = [pltpu.VMEM((6, depth, nb), jnp.bfloat16)]
    if not split_left and not keep:
        scratch.append(pltpu.VMEM((6, mb, depth), jnp.bfloat16))
    if fetch:
        every = [pieces for steps in picks.values() for pieces in steps]
        wide = max(v.shape[2] for v in rights)
        scratch.append(pltpu.VMEM((2, max(sum(e[2] for e in v) for v in every), wide), jnp.float32))
        scratch.append(pltpu.SemaphoreType.DMA((max(len(v) for v in every),)))
    body = functools.partial(
        product_kernel, picks=picks, lefts=len(lefts), rights=len(rights), more=base is not None, halves=halves, fetch=fetch,
        depth=depth, keep=keep, negate=negate,
    )
    steps = rows // mb // min(halves, 2)
    counts = (2, 1, 1) if halves == 3 else (2,) * halves
    out_specs = [
        pl.BlockSpec(
            (c, mb, nb),
            lambda j, i, r, h=min(h, 1): (0, jnp.clip(i - h * steps, 0, steps - 1) * on(r), j * on(r)),
        )
        for h, c in enumerate(counts)
    ]
    out_shape = [jax.ShapeDtypeStruct((c, steps * mb, columns), jnp.float32) for c in counts]
    if keep:
        out_specs.append(pl.BlockSpec((6, mb, total), lambda j, i, r: (0, i, 0)))
        out_shape.append(jax.ShapeDtypeStruct((6, rows, total), jnp.bfloat16))
    result = pl.pallas_call(
        body,
        grid_spec=pltpu.PrefetchScalarGridSpec(
            num_scalar_prefetch=1,
            grid=(columns // nb, rows // mb),
            in_specs=in_specs,
            out_specs=out_specs,
            scratch_shapes=scratch,
        ),
        out_shape=out_shape,
        compiler_params=pltpu.CompilerParams(vmem_limit_bytes=58 * 2**20),
        cost_estimate=pl.CostEstimate(flops=1000, bytes_accessed=1000, transcendentals=0),
    )(role, *args)
    return tuple(result) if len(result) > 1 else result[0]


def place_kernel(role_ref, *refs):
    totals, gots, tops, crossed, out = refs[:2], refs[2:5], refs[5:9], refs[9:13], refs[13]
    f, j = pl.program_id(0), pl.program_id(1)
    kept = role_ref[1] == f
    for role, ref in enumerate(totals):

        @pl.when(kept & (role_ref[0] == role))
        def _():
            out[:, 0] = ref[...]

    @pl.when(jnp.logical_not(kept) & (role_ref[0] == 0))
    def _():
        out[:, 0] = gots[0][...]

    @pl.when(jnp.logical_not(kept) & (role_ref[0] == 1))
    def _():
        out[0, 0], out[1, 0] = gots[1][0], gots[2][0]

    for sources, flag in ((tops, kept), (crossed, jnp.logical_not(kept))):
        for step, ref in enumerate(sources):

            @pl.when(flag & (role_ref[0] >= 2) & (j == step))
            def _():
                out[:, 0] = ref[...]


def place(role, totals, gots, tops, crossed):
    _, rows, columns = totals[0].shape
    w, steps = columns // CHUNKS, 2
    block = rows // steps

    def wide(role_, first, count):
        def at(f, j, i, r):
            used = jnp.where((r[0] == role_) & ((r[1] == f) == first), 1, 0)
            return (0, i * used, j * used)

        return pl.BlockSpec((count, block, w), at)

    def narrow(step, first):
        def at(f, j, i, r):
            used = jnp.where((r[0] >= 2) & ((r[1] == f) == first) & (j == step), 1, 0)
            return (0, i * used, 0)

        return pl.BlockSpec((2, block, w), at)

    uses = ((0, True, 2), (1, True, 2), (0, False, 2), (1, False, 1), (1, False, 1))
    in_specs = [wide(*use) for use in uses]
    in_specs += [narrow(step, first) for first in (True, False) for step in range(CHUNKS)]
    return pl.pallas_call(
        place_kernel,
        grid_spec=pltpu.PrefetchScalarGridSpec(
            num_scalar_prefetch=1,
            grid=(2, CHUNKS, steps),
            in_specs=in_specs,
            out_specs=pl.BlockSpec((2, 1, block, w), lambda f, j, i, r: (0, f, i, (j + 2 * f) % CHUNKS)),
        ),
        out_shape=jax.ShapeDtypeStruct((2, 2, rows, columns), jnp.float32),
        compiler_params=pltpu.CompilerParams(vmem_limit_bytes=40 * 2**20),
        cost_estimate=pl.CostEstimate(flops=1000, bytes_accessed=1000, transcendentals=0),
    )(role, *totals, *gots, *tops, *crossed)


def blocked(recorded):
    row, col = lax.axis_index("row"), lax.axis_index("col")
    z, x, y, c = row // 2, row % 2, col // 2, col % 2
    half, p = z // 2, z % 2
    diag, first, lane = y == half, c == p, c == half
    at_end = (z == 0) | (z == 3)
    role = jnp.where(diag, jnp.where(first, 0, 1), jnp.where(lane, 3, 2) + jnp.where(at_end, 0, 2)).astype(jnp.int32)
    roles = jnp.reshape(role, (1,))
    part, width = recorded.shape[2], recorded.shape[3]
    w, n = width // CHUNKS, width

    def send(value, *moves):
        pairs = []
        for zz in range(4):
            for xx in range(2):
                for yy in range(2):
                    for cc in range(2):
                        for move in moves:
                            to = move(zz, xx, yy, cc)
                            if to is not None:
                                a, b, d, e = to
                                pairs.append((((zz * 2 + xx) * 2 + yy) * 2 + cc, ((a * 2 + b) * 2 + d) * 2 + e))
        return lax.ppermute(value, AXES, pairs)

    def on_diag(zz, yy):
        return yy == zz // 2

    swap_x = lambda a, b, d, e: (a, 1 - b, d, e)
    swap_y = lambda a, b, d, e: (a, b, 1 - d, e)
    swap_core = lambda a, b, d, e: (a, b, d, 1 - e)
    swap_core_diag = lambda a, b, d, e: (a, b, d, 1 - e) if on_diag(a, d) else None
    to_diag = lambda a, b, d, e: None if on_diag(a, d) else (a, b, 1 - d, e)
    to_off = lambda a, b, d, e: (a, b, 1 - d, e) if on_diag(a, d) else None
    swap_slab = lambda a, b, d, e: (a ^ 1, b, d, e) if on_diag(a, d) else None
    first_to_slab = lambda a, b, d, e: (a ^ 1, b, d, e) if on_diag(a, d) and e == a % 2 else None
    over_middle = lambda a, b, d, e: (3 - a, b, d, e) if on_diag(a, d) and a in (1, 2) else None
    middle_second = lambda a, b, d, e: (3 - a, b, d, e) if on_diag(a, d) and a in (1, 2) and e != a % 2 else None
    outward = lambda a, b, d, e: {1: (0, b, d, e), 2: (3, b, d, e)}.get(a) if not on_diag(a, d) else None
    outward_second = lambda a, b, d, e: outward(a, b, d, e) if e != a // 2 else None
    x_first = lambda a, b, d, e: (a, 1 - b, d, e) if on_diag(a, d) and e == a % 2 else None
    x_second = lambda a, b, d, e: (a, 1 - b, d, e) if on_diag(a, d) and e != a % 2 else None
    x_off = lambda a, b, d, e: None if on_diag(a, d) else (a, 1 - b, d, e)

    pick = jnp.where
    sync = lambda *values: lax.optimization_barrier(values)
    mid_off = jnp.logical_not(diag | at_end)

    def cut(f, j):
        start = (j * w + f * part) % width
        return lax.dynamic_slice(recorded, (0, f, 0, start), (2, 1, part, 2 * w))[:, 0]

    def chunk(value, j):
        return value[:, :, j * w : (j + 1) * w]

    mine, give = [cut(x, 0), cut(x, 2)], [cut(1 - x, 0), cut(1 - x, 2)]
    got = send(give[0], swap_x)
    own01 = jnp.concatenate([mine[0], got], 1)
    own = [chunk(own01, 0), chunk(own01, 1)]
    lows = jnp.concatenate([own[0], own[1][:, w:]], 1)
    own01, own[0], own[1], lows, give[1] = sync(own01, own[0], own[1], lows, give[1])

    right, there, seen, cores, seen_cores = [None] * 4, [None] * 4, [None] * 4, [None] * 4, [None] * 4
    got = send(give[1], swap_x)
    right[0] = send(own[0], to_diag, over_middle)
    low01 = send(lows, first_to_slab)
    core01 = send(own01, swap_core)
    own23 = jnp.concatenate([mine[1], got], 1)
    own += [chunk(own23, 0), chunk(own23, 1)]
    lows23 = jnp.concatenate([own[2][:, 2 * w :], own[3][:, 3 * w :]], 1)
    mixed = pick(diag & first, jnp.concatenate([own[1][:, w:], own[3][:, 3 * w :]], 1), own[1])
    own23, own[2], own[3], lows23, mixed, right[0], low01, core01 = sync(
        own23, own[2], own[3], lows23, mixed, right[0], low01, core01
    )
    core23 = send(own23, swap_core)

    def whole(which, k, row, transposed=False):
        return (which, 0, k, transposed, row, 0)

    def lower(sources, j, row, col):
        out = [(sources[i][0], sources[i][1] + (j - i) * w, w, True, row + i * w, col) for i in range(j)]
        return out + [(sources[j][0], sources[j][1], n - j * w, False, row + j * w, col)]

    there[0] = send(right[0], swap_slab, outward)
    right[1] = send(mixed, to_diag, over_middle)
    low23 = send(lows23, first_to_slab)
    cores[0] = send(right[0], swap_core_diag)
    both = [whole(0, n, 0, True), whole(1, n, n // 2, True)]
    total, left = product(
        roles,
        [own01, own23, core01, core23],
        [core01, core23, own01, own23],
        {0: [both], 1: [[whole(2, n, 0), (3, 0, n, False, 0, n // 2)]]},
        n,
        fetch=True,
        keep=True,
    )
    there[0], right[1], total, left = sync(there[0], right[1], total, left)
    mixed = pick(diag & first, chunk(core23, 1), own[2])
    seen[0] = pick(mid_off, right[0], there[0])
    there[0], right[1], low01, low23, cores[0], left, total, mixed, seen[0], own[3] = sync(
        there[0], right[1], low01, low23, cores[0], left, total, mixed, seen[0], own[3]
    )

    def share(j):
        r, t = right[j], there[j]
        return product(
            roles, left, [r, t], {0: [[whole(0, n, 0), whole(1, n, n)]], 1: [[whole(1, n, 0), whole(0, n, n)]]}, w, fetch=True
        )

    def add_rights(total, js, active, halves=1):
        these = [right[j] for j in js] + [cores[j] for j in js]
        others = [there[j] for j in js] + [seen_cores[j] for j in js]
        k = len(these)
        rights = (these if 0 in active else []) + (others if 1 in active else [])
        first_of = {0: 0, 1: len(rights) - k}
        picks = {v: [[whole(first_of[v] + i, n, i * w, True) for i in range(k)]] for v in active}
        return product(roles, these, rights, picks, n, base=total, halves=halves, fetch=True, negate=halves > 1)

    shares, shared = [None] * 4, [None] * 4
    there[1] = send(right[1], swap_slab, outward)
    right[2] = send(mixed, to_diag, over_middle)
    cores[1] = send(right[1], swap_core_diag)
    seen_cores[0] = send(seen[0], swap_core)
    shares[0] = share(0)
    low_sources = [(2, 0), (2, n), (3, 0), (3, 2 * w)]
    total = product(
        roles,
        left,
        [own01, own23, low01, low23],
        {0: [both], 1: [sum([lower(low_sources, j, 0, j * w) for j in range(4)], [])]},
        n,
        base=total,
        half=0,
        fetch=True,
    )
    mixed = pick(diag, shares[0], own[3])
    seen[1] = pick(mid_off, right[1], there[1])
    there[1], right[2], low01, low23, cores[1], seen_cores[0], total, mixed, seen[1] = sync(
        there[1], right[2], low01, low23, cores[1], seen_cores[0], total, mixed, seen[1]
    )

    there[2] = send(right[2], swap_slab, outward)
    right[3] = send(mixed, swap_y)
    near3 = send(low01, middle_second)
    cores[2] = send(right[2], swap_core_diag)
    seen_cores[1] = send(seen[1], swap_core)
    shares[1] = share(1)
    shares[1], seen_cores[1], cores[1], total = sync(shares[1], seen_cores[1], cores[1], total)
    total = add_rights(total, (0, 1), (0, 1))
    seen[2] = pick(mid_off, right[2], there[2])
    mixed = pick(diag & first, lows23, low23)
    swapped = pick(diag, right[3], seen[2])
    there[2], right[3], near3, cores[2], shares[1], total, swapped, mixed = sync(
        there[2], right[3], near3, cores[2], shares[1], total, swapped, mixed
    )
    shared[0] = right[3]

    there[3] = send(right[3], swap_slab)
    shared[1] = send(shares[1], to_off)
    near4 = send(mixed, over_middle)
    far3 = send(near3, outward_second)
    swapped = send(swapped, swap_core)
    shares[2] = share(2)
    shares[2], total, swapped = sync(shares[2], total, swapped)
    cores[3] = swapped
    keep_first, to_first = add_rights(total, (2, 3), (0,), 2)
    to_first, swapped, far3, near3 = sync(to_first, swapped, far3, near3)

    far4 = near4

    def rest(j, base):
        rights = seen[:3] + seen_cores[:2] + [swapped, far3, far4, near3, near4]
        picks = {}
        for k, last in ((2, 6), (4, 8)):
            lane_low = [(0, 0), (1, 0), (last + 1, 0), (1, 3 * w)]
            other_low = [(last, 0), (last, n), (last + 1, 0), (last + 1, 2 * w)]
            picks[k] = lower(other_low, j, 0, 0) + [whole((0, 1, 2, 5)[j], n, n)]
            picks[k + 1] = lower(lane_low, j, 0, 0)
            picks[k + 1] += [(v, j * w, w, True, n + i * w, 0) for i, v in enumerate((3, 4, 5, 2))]
        used = sorted({entry[0] for pieces in picks.values() for entry in pieces})
        picks = {r: [[(used.index(e[0]),) + e[1:] for e in v]] for r, v in picks.items()}
        return product(roles, left, [rights[i] for i in used], picks, w, base=base, halves=2, fetch=True, negate=True)

    tops, downs, crossed = [None] * 4, [None] * 4, [None] * 4
    tops[0], downs[0] = rest(0, shared[0])
    there[3], shared[1], near4, far3, swapped, shares[2], keep_first, to_first, total, downs[0] = sync(
        there[3], shared[1], near4, far3, swapped, shares[2], keep_first, to_first, total, downs[0]
    )

    far4 = send(near4, outward)
    shared[2] = send(shares[2], to_off)
    seen_cores[2] = send(there[2], swap_core_diag)
    got_first = send(to_first, x_first)
    seen_cores[3] = send(there[3], swap_core_diag)
    crossed[0] = send(downs[0], x_off)
    shares[3] = share(3)
    shares[3], shared[1], seen_cores[2], seen_cores[3] = sync(shares[3], shared[1], seen_cores[2], seen_cores[3])
    shared[3] = send(shares[3], to_off)
    tops[1], downs[1] = rest(1, shared[1])
    downs[1], total, crossed[0] = sync(downs[1], total, crossed[0])
    crossed[1] = send(downs[1], x_off)
    keep_second, *to_second = add_rights(total, (2, 3), (1,), 3)
    to_second[0], to_second[1], shared[2], far4 = sync(*to_second, shared[2], far4)
    got_second = [send(v, x_second) for v in to_second]
    tops[2], downs[2] = rest(2, shared[2])
    downs[2], crossed[1], got_first, far3 = sync(downs[2], crossed[1], got_first, far3)
    crossed[2] = send(downs[2], x_off)
    tops[3], downs[3] = rest(3, None)
    tops[3], downs[3], shared[3], crossed[2] = sync(tops[3], downs[3], shared[3], crossed[2])
    downs[3] = downs[3] - shared[3][:, part:]
    crossed[3] = send(downs[3], x_off)
    tops[3] = tops[3] - shared[3][:, :part]

    flags = jnp.stack([role, x.astype(jnp.int32)])
    return place(flags, [keep_first, keep_second], [got_first] + got_second, tops, crossed)


def solution(mesh):
    rows, cols = mesh.shape["row"], mesh.shape["col"]

    def body(recorded):
        frequencies = recorded.shape[1]
        if frequencies == 2 and cols == 4 and rows == frequencies * cols:
            return blocked(recorded)
        return gathered(recorded)

    spec = P(None, None, "row", "col")
    return jax.shard_map(body, mesh=mesh, in_specs=(spec,), out_specs=spec, check_vma=False)
```

```python
import functools

import jax
import jax.numpy as jnp
from jax import lax
from jax.experimental import pallas as pl
from jax.experimental.pallas import tpu as pltpu
from jax.sharding import PartitionSpec as P

AXES = ("row", "col")
CHUNKS = 4


def dot(left, right):
    return jnp.dot(left, right, precision=lax.Precision.HIGH, preferred_element_type=jnp.float32)


def multiply_complex(left, right):
    rr, ii = dot(left[0], right[0]), dot(left[1], right[1])
    ss = dot(left[0] + left[1], right[0] + right[1])
    return jnp.stack([rr - ii, ss - rr - ii])


def gathered(recorded):
    rows = lax.all_gather(recorded, "col", axis=3, tiled=True)
    columns = lax.all_gather(recorded, "row", axis=2, tiled=True)
    out = [multiply_complex(rows[:, f], columns[:, f]) for f in range(recorded.shape[1])]
    return -jnp.stack(out, axis=1)


def split(value):
    high = value.astype(jnp.bfloat16)
    return high, (value - high.astype(jnp.float32)).astype(jnp.bfloat16)


def split_into(out, at, block, rows=slice(None)):
    k = block[0].shape[1]
    for c in range(3):
        v = block[c] if c < 2 else block[0] + block[1]
        out[2 * c, rows, at : at + k], out[2 * c + 1, rows, at : at + k] = split(v)


def product_kernel(role_ref, *refs, picks, lefts, rights, more, halves, fetch, depth, keep, negate, by_rows):
    left, candidates, rest = refs[:lefts], refs[lefts : lefts + rights], refs[lefts + rights :]
    base, rest = (rest[0], rest[1:]) if more else (None, rest)
    outs, rest = rest[:halves], rest[halves:]
    kept, rest = (rest[0], rest[1:]) if keep else (None, rest)
    scratch = rest[0]
    j, i = pl.program_id(0), pl.program_id(1)
    for role, steps in picks.items():
        for step, pieces in enumerate(steps):

            @pl.when((role_ref[0] == role) & (i == 0) & (j == step))
            def _():
                if fetch:
                    staged, sems = rest[-2:]
                    at, copies = 0, []
                    for which, start, size, _, _, _ in pieces:
                        source = candidates[which].at[:, pl.ds(start, size), :]
                        k = source.shape[2]
                        target = staged.at[:, pl.ds(at, size), pl.ds(0, k)]
                        copies.append(pltpu.make_async_copy(source, target, sems.at[len(copies)]))
                        copies[-1].start()
                        at += size
                    at = 0
                for number, (which, start, size, flip, row, col) in enumerate(pieces):
                    if fetch:
                        copies[number].wait()
                        k = candidates[which].shape[2]
                        block = [staged[c, at : at + size, :k] for c in range(2)]
                        at += size
                    else:
                        block = [candidates[which][c, start : start + size, :] for c in range(2)]
                    if flip:
                        block = [v.T for v in block]
                    split_into(scratch, col, block, slice(row, row + block[0].shape[0]))

    def split_left(held):
        at = 0
        for ref in left:
            split_into(held, at, ref)
            at += ref.shape[2]

    if keep:
        split_left(kept)

    @pl.when(functools.reduce(jnp.logical_or, [role_ref[0] == role for role in picks]))
    def _():
        if keep:
            parts = multiply_split(kept, slice(kept.shape[2] - depth, None), scratch, by_rows)
        elif lefts == 1:
            parts = multiply_split(left[0], slice(None), scratch, by_rows)
        else:
            split_left(rest[1])
            parts = multiply_split(rest[1], slice(None), scratch, by_rows)
        for h, out in enumerate(outs):

            @pl.when(i * min(halves, 2) // pl.num_programs(1) == min(h, 1))
            def _():
                for at, c in enumerate((h - 1,) if halves == 3 and h else (0, 1)):
                    value = parts[c] if base is None else parts[c] + base[c]
                    out[at] = -value if negate else value


def multiply(left, right, by_rows):
    dims = (((1,), (1 if by_rows else 0,)), ((), ()))
    return lax.dot_general(left, right, dims, preferred_element_type=jnp.float32)


def multiply_split(left, columns, right, by_rows):
    parts = []
    for c in range(3):
        high, low = left[2 * c, :, columns], left[2 * c + 1, :, columns]
        total = multiply(high, right[2 * c], by_rows)
        total += multiply(high, right[2 * c + 1], by_rows)
        total += multiply(low, right[2 * c], by_rows)
        parts.append(total)
    rr, ii, ss = parts
    return rr - ii, ss - rr - ii


def product(role, left, rights, picks, columns, base=None, half=None, halves=1, fetch=False, keep=False, negate=False, by_rows=False):
    split_left = not isinstance(left, list)
    lefts = [left] if split_left else left
    rows = lefts[0].shape[1]
    total = sum(v.shape[2] for v in lefts)
    depth = total // (1 if half is None and not keep else 2)
    mb, nb = rows // CHUNKS, columns
    once = pl.Buffered(1)

    def on(r):
        return functools.reduce(jnp.maximum, [jnp.where(r[0] == role_, 1, 0) for role_ in picks])

    if split_left:
        in_specs = [pl.BlockSpec((6, mb, depth), lambda j, i, r: (0, i * on(r), half or 0))]
    else:
        in_specs = [
            pl.BlockSpec((2, mb, v.shape[2]), lambda j, i, r: (0, i * (1 if keep else on(r)), 0)) for v in lefts
        ]
    arrays = []
    for v in rights:
        if fetch:
            arrays.append(v)
            spec = pl.BlockSpec(memory_space=pl.ANY)
        elif isinstance(v, tuple):
            arrays.append(v[0])
            spec = pl.BlockSpec((2, nb, v[0].shape[2]), lambda j, i, r: (0, j * on(r), 0), pipeline_mode=once)
        else:
            arrays.append(v)
            spec = pl.BlockSpec(v.shape, lambda j, i, r: (0, 0, 0), pipeline_mode=once)
        in_specs.append(spec)
    args = lefts + arrays
    if base is not None:
        in_specs.append(pl.BlockSpec((2, mb, nb), lambda j, i, r: (0, i * on(r), j * on(r))))
        args.append(base)
    scratch = [pltpu.VMEM((6, nb, depth) if by_rows else (6, depth, nb), jnp.bfloat16)]
    if not split_left and not keep:
        scratch.append(pltpu.VMEM((6, mb, depth), jnp.bfloat16))
    if fetch:
        every = [pieces for steps in picks.values() for pieces in steps]
        wide = max(v.shape[2] for v in rights)
        scratch.append(pltpu.VMEM((2, max(sum(e[2] for e in v) for v in every), wide), jnp.float32))
        scratch.append(pltpu.SemaphoreType.DMA((max(len(v) for v in every),)))
    body = functools.partial(
        product_kernel, picks=picks, lefts=len(lefts), rights=len(rights), more=base is not None, halves=halves, fetch=fetch,
        depth=depth, keep=keep, negate=negate, by_rows=by_rows,
    )
    steps = rows // mb // min(halves, 2)
    counts = (2, 1, 1) if halves == 3 else (2,) * halves
    out_specs = [
        pl.BlockSpec(
            (c, mb, nb),
            lambda j, i, r, h=min(h, 1): (0, jnp.clip(i - h * steps, 0, steps - 1) * on(r), j * on(r)),
        )
        for h, c in enumerate(counts)
    ]
    out_shape = [jax.ShapeDtypeStruct((c, steps * mb, columns), jnp.float32) for c in counts]
    if keep:
        out_specs.append(pl.BlockSpec((6, mb, total), lambda j, i, r: (0, i, 0)))
        out_shape.append(jax.ShapeDtypeStruct((6, rows, total), jnp.bfloat16))
    result = pl.pallas_call(
        body,
        grid_spec=pltpu.PrefetchScalarGridSpec(
            num_scalar_prefetch=1,
            grid=(columns // nb, rows // mb),
            in_specs=in_specs,
            out_specs=out_specs,
            scratch_shapes=scratch,
        ),
        out_shape=out_shape,
        compiler_params=pltpu.CompilerParams(vmem_limit_bytes=58 * 2**20),
        cost_estimate=pl.CostEstimate(flops=1000, bytes_accessed=1000, transcendentals=0),
    )(role, *args)
    return tuple(result) if len(result) > 1 else result[0]


def place_kernel(role_ref, *refs):
    blocks, out = refs[: 4 + CHUNKS], refs[-1]
    for role, sources in ((0, blocks[:1]), (1, blocks[1:4])):

        @pl.when(role_ref[0] == role)
        def _():
            if sources[-1].shape[0] == 2:
                out[:, 0] = sources[0][...]
            else:
                out[0, 0], out[1, 0] = sources[1][0], sources[2][0]

    for step, ref in enumerate(blocks[4:]):

        @pl.when((role_ref[0] >= 2) & (pl.program_id(0) == step))
        def _():
            out[:, 0] = ref[...]


def place(role, first, second, chunks, other, onto=None):
    _, rows, columns = first.shape
    w, steps = columns // CHUNKS, 2
    block = rows // steps
    second = [second] * 3 if not isinstance(second, list) else [second[0]] + second

    def wide(role_, count):
        def at(j, i, r):
            used = jnp.where(r[0] == role_, 1, 0)
            return (0, i * used, j * used)

        return pl.BlockSpec((count, block, w), at)

    def narrow(step):
        return pl.BlockSpec((2, block, w), lambda j, i, r: (0, i * jnp.where((r[0] >= 2) & (j == step), 1, 0), 0))

    def to(j, i, r):
        f = 1 - r[1] if other else r[1]
        return (0, f, i, (j + 2 * f) % CHUNKS)

    in_specs = [wide(0, 2)] + [wide(1, v.shape[0]) for v in second] + [narrow(step) for step in range(CHUNKS)]
    args = [role, first, *second, *chunks]
    if other:
        in_specs.append(pl.BlockSpec(memory_space=pl.ANY))
        args.append(onto)
    return pl.pallas_call(
        place_kernel,
        grid_spec=pltpu.PrefetchScalarGridSpec(
            num_scalar_prefetch=1,
            grid=(CHUNKS, steps),
            in_specs=in_specs,
            out_specs=pl.BlockSpec((2, 1, block, w), to),
        ),
        out_shape=jax.ShapeDtypeStruct((2, 2, rows, columns), jnp.float32),
        input_output_aliases={len(args) - 1: 0} if other else {},
        compiler_params=pltpu.CompilerParams(vmem_limit_bytes=40 * 2**20),
        cost_estimate=pl.CostEstimate(flops=1000, bytes_accessed=1000, transcendentals=0),
    )(*args)


def blocked(recorded):
    row, col = lax.axis_index("row"), lax.axis_index("col")
    z, x, y, c = row // 2, row % 2, col // 2, col % 2
    half, p = z // 2, z % 2
    diag, first, lane = y == half, c == p, c == half
    at_end = (z == 0) | (z == 3)
    role = jnp.where(diag, jnp.where(first, 0, 1), jnp.where(lane, 3, 2) + jnp.where(at_end, 0, 2)).astype(jnp.int32)
    roles = jnp.reshape(role, (1,))
    part, width = recorded.shape[2], recorded.shape[3]
    w, n = width // CHUNKS, width

    def send(value, *moves):
        pairs = []
        for zz in range(4):
            for xx in range(2):
                for yy in range(2):
                    for cc in range(2):
                        for move in moves:
                            to = move(zz, xx, yy, cc)
                            if to is not None:
                                a, b, d, e = to
                                pairs.append((((zz * 2 + xx) * 2 + yy) * 2 + cc, ((a * 2 + b) * 2 + d) * 2 + e))
        return lax.ppermute(value, AXES, pairs)

    def on_diag(zz, yy):
        return yy == zz // 2

    swap_x = lambda a, b, d, e: (a, 1 - b, d, e)
    swap_y = lambda a, b, d, e: (a, b, 1 - d, e)
    swap_core = lambda a, b, d, e: (a, b, d, 1 - e)
    swap_core_diag = lambda a, b, d, e: (a, b, d, 1 - e) if on_diag(a, d) else None
    to_diag = lambda a, b, d, e: None if on_diag(a, d) else (a, b, 1 - d, e)
    to_off = lambda a, b, d, e: (a, b, 1 - d, e) if on_diag(a, d) else None
    swap_slab = lambda a, b, d, e: (a ^ 1, b, d, e) if on_diag(a, d) else None
    first_to_slab = lambda a, b, d, e: (a ^ 1, b, d, e) if on_diag(a, d) and e == a % 2 else None
    over_middle = lambda a, b, d, e: (3 - a, b, d, e) if on_diag(a, d) and a in (1, 2) else None
    middle_second = lambda a, b, d, e: (3 - a, b, d, e) if on_diag(a, d) and a in (1, 2) and e != a % 2 else None
    outward = lambda a, b, d, e: {1: (0, b, d, e), 2: (3, b, d, e)}.get(a) if not on_diag(a, d) else None
    outward_second = lambda a, b, d, e: outward(a, b, d, e) if e != a // 2 else None
    x_first = lambda a, b, d, e: (a, 1 - b, d, e) if on_diag(a, d) and e == a % 2 else None
    x_second = lambda a, b, d, e: (a, 1 - b, d, e) if on_diag(a, d) and e != a % 2 else None
    x_off = lambda a, b, d, e: None if on_diag(a, d) else (a, 1 - b, d, e)

    pick = jnp.where
    sync = lambda *values: lax.optimization_barrier(values)
    mid_off = jnp.logical_not(diag | at_end)

    def cut(f, j):
        start = (j * w + f * part) % width
        return lax.dynamic_slice(recorded, (0, f, 0, start), (2, 1, part, 2 * w))[:, 0]

    def chunk(value, j):
        return value[:, :, j * w : (j + 1) * w]

    mine, give = [cut(x, 0), cut(x, 2)], [cut(1 - x, 0), cut(1 - x, 2)]
    got = send(give[0], swap_x)
    own01 = jnp.concatenate([mine[0], got], 1)
    own = [chunk(own01, 0), chunk(own01, 1)]
    lows = jnp.concatenate([own[0], own[1][:, w:]], 1)
    own01, own[0], own[1], lows, give[1] = sync(own01, own[0], own[1], lows, give[1])

    right, there, seen, cores, seen_cores = [None] * 4, [None] * 4, [None] * 4, [None] * 4, [None] * 4
    got = send(give[1], swap_x)
    right[0] = send(own[0], to_diag, over_middle)
    low01 = send(lows, first_to_slab)
    core01 = send(own01, swap_core)
    own23 = jnp.concatenate([mine[1], got], 1)
    own += [chunk(own23, 0), chunk(own23, 1)]
    lows23 = jnp.concatenate([own[2][:, 2 * w :], own[3][:, 3 * w :]], 1)
    mixed = pick(diag & first, jnp.concatenate([own[1][:, w:], own[3][:, 3 * w :]], 1), own[1])
    own23, own[2], own[3], lows23, mixed, right[0], low01, core01 = sync(
        own23, own[2], own[3], lows23, mixed, right[0], low01, core01
    )
    core23 = send(own23, swap_core)

    def whole(which, k, row, transposed=False):
        return (which, 0, k, transposed, row, 0)

    def lower(sources, j, row, col):
        out = [(sources[i][0], sources[i][1] + (j - i) * w, w, True, row + i * w, col) for i in range(j)]
        return out + [(sources[j][0], sources[j][1], n - j * w, False, row + j * w, col)]

    there[0] = send(right[0], swap_slab, outward)
    right[1] = send(mixed, to_diag, over_middle)
    low23 = send(lows23, first_to_slab)
    cores[0] = send(right[0], swap_core_diag)
    both = [whole(0, n, 0, True), whole(1, n, n // 2, True)]
    total, left = product(
        roles,
        [own01, own23, core01, core23],
        [core01, core23, own01, own23],
        {0: [both], 1: [[whole(2, n, 0), (3, 0, n, False, 0, n // 2)]]},
        n,
        fetch=True,
        keep=True,
    )
    there[0], right[1], total, left = sync(there[0], right[1], total, left)
    there[1] = send(right[1], swap_slab, outward)
    mixed = pick(diag & first, chunk(core23, 1), own[2])
    seen[0] = pick(mid_off, right[0], there[0])
    there[0], right[1], low01, low23, cores[0], left, total, mixed, seen[0], own[3] = sync(
        there[0], right[1], low01, low23, cores[0], left, total, mixed, seen[0], own[3]
    )

    def share(j):
        r, t = right[j], there[j]
        return product(
            roles, left, [r, t], {0: [[whole(0, n, 0), whole(1, n, n)]], 1: [[whole(1, n, 0), whole(0, n, n)]]}, w
        )

    def add_rights(total, js, active, halves=1):
        these = [right[j] for j in js] + [cores[j] for j in js]
        others = [there[j] for j in js] + [seen_cores[j] for j in js]
        k = len(these)
        rights = (these if 0 in active else []) + (others if 1 in active else [])
        first_of = {0: 0, 1: len(rights) - k}
        picks = {v: [[(first_of[v] + i, 0, n, False, 0, i * w) for i in range(k)]] for v in active}
        return product(roles, these, rights, picks, n, base=total, halves=halves, fetch=True, negate=halves > 1, by_rows=True)

    shares, shared = [None] * 4, [None] * 4
    right[2] = send(mixed, to_diag, over_middle)
    cores[1] = send(right[1], swap_core_diag)
    seen_cores[0] = send(seen[0], swap_core)
    shares[0] = share(0)
    low_sources = [(2, 0), (2, n), (3, 0), (3, 2 * w)]
    total = product(
        roles,
        left,
        [own01, own23, low01, low23],
        {
            0: [[(0, 0, n, False, 0, 0), (1, 0, n, False, 0, n // 2)]],
            1: [sum([lower(low_sources, j, 0, j * w) for j in range(4)], [])],
        },
        n,
        base=total,
        half=0,
        fetch=True,
        by_rows=True,
    )
    right[2], total = sync(right[2], total)
    there[2] = send(right[2], swap_slab, outward)
    mixed = pick(diag, shares[0], own[3])
    seen[1] = pick(mid_off, right[1], there[1])
    there[1], right[2], low01, low23, cores[1], seen_cores[0], total, mixed, seen[1] = sync(
        there[1], right[2], low01, low23, cores[1], seen_cores[0], total, mixed, seen[1]
    )

    right[3] = send(mixed, swap_y)
    near3 = send(low01, middle_second)
    cores[2] = send(right[2], swap_core_diag)
    seen_cores[1] = send(seen[1], swap_core)
    shares[1] = share(1)
    shares[1], seen_cores[1], cores[1], total = sync(shares[1], seen_cores[1], cores[1], total)
    total = add_rights(total, (0, 1), (0, 1))
    right[3], total = sync(right[3], total)
    there[3] = send(right[3], swap_slab)
    seen[2] = pick(mid_off, right[2], there[2])
    mixed = pick(diag & first, lows23, low23)
    swapped = pick(diag, right[3], seen[2])
    there[2], right[3], near3, cores[2], shares[1], total, swapped, mixed = sync(
        there[2], right[3], near3, cores[2], shares[1], total, swapped, mixed
    )
    shared[0] = right[3]

    shared[1] = send(shares[1], to_off)
    near4 = send(mixed, over_middle)
    far3 = send(near3, outward_second)
    swapped = send(swapped, swap_core)
    shares[2] = share(2)
    shares[2], total, swapped = sync(shares[2], total, swapped)
    cores[3] = swapped
    keep_first, to_first = add_rights(total, (2, 3), (0,), 2)
    to_first, swapped, far3, near3 = sync(to_first, swapped, far3, near3)

    far4 = near4

    def rest(j, base):
        rights = seen[:3] + seen_cores[:2] + [swapped, far3, far4, near3, near4]
        picks = {}
        for k, last in ((2, 6), (4, 8)):
            lane_low = [(0, 0), (1, 0), (last + 1, 0), (1, 3 * w)]
            other_low = [(last, 0), (last, n), (last + 1, 0), (last + 1, 2 * w)]
            picks[k] = lower(other_low, j, 0, 0) + [whole((0, 1, 2, 5)[j], n, n)]
            picks[k + 1] = lower(lane_low, j, 0, 0)
            picks[k + 1] += [(v, j * w, w, True, n + i * w, 0) for i, v in enumerate((3, 4, 5, 2))]
        used = sorted({entry[0] for pieces in picks.values() for entry in pieces})
        picks = {r: [[(used.index(e[0]),) + e[1:] for e in v]] for r, v in picks.items()}
        return product(roles, left, [rights[i] for i in used], picks, w, base=base, halves=2, fetch=True, negate=True)

    tops, downs, crossed = [None] * 4, [None] * 4, [None] * 4
    tops[0], downs[0] = rest(0, shared[0])
    there[3], shared[1], near4, far3, swapped, shares[2], keep_first, to_first, total, downs[0] = sync(
        there[3], shared[1], near4, far3, swapped, shares[2], keep_first, to_first, total, downs[0]
    )

    far4 = send(near4, outward)
    shared[2] = send(shares[2], to_off)
    seen_cores[2] = send(there[2], swap_core_diag)
    got_first = send(to_first, x_first)
    seen_cores[3] = send(there[3], swap_core_diag)
    crossed[0] = send(downs[0], x_off)
    shares[3] = share(3)
    shares[3], shared[1], seen_cores[2], seen_cores[3] = sync(shares[3], shared[1], seen_cores[2], seen_cores[3])
    shared[3] = send(shares[3], to_off)
    tops[1], downs[1] = rest(1, shared[1])
    downs[1], total, crossed[0] = sync(downs[1], total, crossed[0])
    crossed[1] = send(downs[1], x_off)
    keep_second, *to_second = add_rights(total, (2, 3), (1,), 3)
    to_second[0], to_second[1], shared[2], far4 = sync(*to_second, shared[2], far4)
    got_second = [send(v, x_second) for v in to_second]
    tops[2], downs[2] = rest(2, shared[2])
    downs[2], crossed[1], got_first, far3 = sync(downs[2], crossed[1], got_first, far3)
    crossed[2] = send(downs[2], x_off)
    tops[3], downs[3] = rest(3, None)
    tops[3], downs[3], shared[3], crossed[2] = sync(tops[3], downs[3], shared[3], crossed[2])
    downs[3] = downs[3] - shared[3][:, part:]
    crossed[3] = send(downs[3], x_off)
    tops[3] = tops[3] - shared[3][:, :part]

    flags = jnp.stack([role, x.astype(jnp.int32)])
    out = place(flags, keep_first, keep_second, tops, False)
    return place(flags, got_first, got_second, crossed, True, out)


def solution(mesh):
    rows, cols = mesh.shape["row"], mesh.shape["col"]

    def body(recorded):
        frequencies = recorded.shape[1]
        if frequencies == 2 and cols == 4 and rows == frequencies * cols:
            return blocked(recorded)
        return gathered(recorded)

    spec = P(None, None, "row", "col")
    return jax.shard_map(body, mesh=mesh, in_specs=(spec,), out_specs=spec, check_vma=False)
```

```python
import functools

import jax
import jax.numpy as jnp
from jax import lax
from jax.experimental import pallas as pl
from jax.experimental.pallas import tpu as pltpu
from jax.sharding import PartitionSpec as P

AXES = ("row", "col")
CHUNKS = 4


def dot(left, right):
    return jnp.dot(left, right, precision=lax.Precision.HIGH, preferred_element_type=jnp.float32)


def multiply_complex(left, right):
    rr, ii = dot(left[0], right[0]), dot(left[1], right[1])
    ss = dot(left[0] + left[1], right[0] + right[1])
    return jnp.stack([rr - ii, ss - rr - ii])


def gathered(recorded):
    rows = lax.all_gather(recorded, "col", axis=3, tiled=True)
    columns = lax.all_gather(recorded, "row", axis=2, tiled=True)
    out = [multiply_complex(rows[:, f], columns[:, f]) for f in range(recorded.shape[1])]
    return -jnp.stack(out, axis=1)


def split(value):
    high = value.astype(jnp.bfloat16)
    return high, (value - high.astype(jnp.float32)).astype(jnp.bfloat16)


def split_into(out, at, block, rows=slice(None)):
    k = block[0].shape[1]
    for c in range(3):
        v = block[c] if c < 2 else block[0] + block[1]
        out[2 * c, rows, at : at + k], out[2 * c + 1, rows, at : at + k] = split(v)


def product_kernel(role_ref, *refs, picks, lefts, rights, more, halves, fetch, depth, keep, negate, by_rows):
    left, candidates, rest = refs[:lefts], refs[lefts : lefts + rights], refs[lefts + rights :]
    base, rest = (rest[0], rest[1:]) if more else (None, rest)
    outs, rest = rest[:halves], rest[halves:]
    kept, rest = (rest[0], rest[1:]) if keep else (None, rest)
    scratch = rest[0]
    j, i = pl.program_id(0), pl.program_id(1)
    for role, steps in picks.items():
        for step, pieces in enumerate(steps):

            @pl.when((role_ref[0] == role) & (i == 0) & (j == step))
            def _():
                if fetch:
                    staged, sems = rest[-2:]
                    at, copies = 0, []
                    for which, start, size, _, _, _ in pieces:
                        source = candidates[which].at[:, pl.ds(start, size), :]
                        k = source.shape[2]
                        target = staged.at[:, pl.ds(at, size), pl.ds(0, k)]
                        copies.append(pltpu.make_async_copy(source, target, sems.at[len(copies)]))
                        copies[-1].start()
                        at += size
                    at = 0
                for number, (which, start, size, flip, row, col) in enumerate(pieces):
                    if fetch:
                        copies[number].wait()
                        k = candidates[which].shape[2]
                        block = [staged[c, at : at + size, :k] for c in range(2)]
                        at += size
                    else:
                        block = [candidates[which][c, start : start + size, :] for c in range(2)]
                    if flip:
                        block = [v.T for v in block]
                    split_into(scratch, col, block, slice(row, row + block[0].shape[0]))

    def split_left(held):
        at = 0
        for ref in left:
            split_into(held, at, ref)
            at += ref.shape[2]

    if keep:
        split_left(kept)

    @pl.when(functools.reduce(jnp.logical_or, [role_ref[0] == role for role in picks]))
    def _():
        if keep:
            parts = multiply_split(kept, slice(kept.shape[2] - depth, None), scratch, by_rows)
        elif lefts == 1:
            parts = multiply_split(left[0], slice(None), scratch, by_rows)
        else:
            split_left(rest[1])
            parts = multiply_split(rest[1], slice(None), scratch, by_rows)
        for h, out in enumerate(outs):

            @pl.when(i * min(halves, 2) // pl.num_programs(1) == min(h, 1))
            def _():
                for at, c in enumerate((h - 1,) if halves == 3 and h else (0, 1)):
                    value = parts[c] if base is None else parts[c] + base[c]
                    out[at] = -value if negate else value


def multiply(left, right, by_rows):
    dims = (((1,), (1 if by_rows else 0,)), ((), ()))
    return lax.dot_general(left, right, dims, preferred_element_type=jnp.float32)


def multiply_split(left, columns, right, by_rows):
    parts = []
    for c in range(3):
        high, low = left[2 * c, :, columns], left[2 * c + 1, :, columns]
        total = multiply(high, right[2 * c], by_rows)
        total += multiply(high, right[2 * c + 1], by_rows)
        total += multiply(low, right[2 * c], by_rows)
        parts.append(total)
    rr, ii, ss = parts
    return rr - ii, ss - rr - ii


def product(role, left, rights, picks, columns, base=None, half=None, halves=1, fetch=False, keep=False, negate=False, by_rows=False):
    split_left = not isinstance(left, list)
    lefts = [left] if split_left else left
    rows = lefts[0].shape[1]
    total = sum(v.shape[2] for v in lefts)
    depth = total // (1 if half is None and not keep else 2)
    mb, nb = rows // CHUNKS, columns
    once = pl.Buffered(1)

    def on(r):
        return functools.reduce(jnp.maximum, [jnp.where(r[0] == role_, 1, 0) for role_ in picks])

    if split_left:
        in_specs = [pl.BlockSpec((6, mb, depth), lambda j, i, r: (0, i * on(r), half or 0))]
    else:
        in_specs = [
            pl.BlockSpec((2, mb, v.shape[2]), lambda j, i, r: (0, i * (1 if keep else on(r)), 0)) for v in lefts
        ]
    arrays = []
    for v in rights:
        if fetch:
            arrays.append(v)
            spec = pl.BlockSpec(memory_space=pl.ANY)
        elif isinstance(v, tuple):
            arrays.append(v[0])
            spec = pl.BlockSpec((2, nb, v[0].shape[2]), lambda j, i, r: (0, j * on(r), 0), pipeline_mode=once)
        else:
            arrays.append(v)
            spec = pl.BlockSpec(v.shape, lambda j, i, r: (0, 0, 0), pipeline_mode=once)
        in_specs.append(spec)
    args = lefts + arrays
    if base is not None:
        in_specs.append(pl.BlockSpec((2, mb, nb), lambda j, i, r: (0, i * on(r), j * on(r))))
        args.append(base)
    scratch = [pltpu.VMEM((6, nb, depth) if by_rows else (6, depth, nb), jnp.bfloat16)]
    if not split_left and not keep:
        scratch.append(pltpu.VMEM((6, mb, depth), jnp.bfloat16))
    if fetch:
        every = [pieces for steps in picks.values() for pieces in steps]
        wide = max(v.shape[2] for v in rights)
        scratch.append(pltpu.VMEM((2, max(sum(e[2] for e in v) for v in every), wide), jnp.float32))
        scratch.append(pltpu.SemaphoreType.DMA((max(len(v) for v in every),)))
    body = functools.partial(
        product_kernel, picks=picks, lefts=len(lefts), rights=len(rights), more=base is not None, halves=halves, fetch=fetch,
        depth=depth, keep=keep, negate=negate, by_rows=by_rows,
    )
    steps = rows // mb // min(halves, 2)
    counts = (2, 1, 1) if halves == 3 else (2,) * halves
    out_specs = [
        pl.BlockSpec(
            (c, mb, nb),
            lambda j, i, r, h=min(h, 1): (0, jnp.clip(i - h * steps, 0, steps - 1) * on(r), j * on(r)),
        )
        for h, c in enumerate(counts)
    ]
    out_shape = [jax.ShapeDtypeStruct((c, steps * mb, columns), jnp.float32) for c in counts]
    if keep:
        out_specs.append(pl.BlockSpec((6, mb, total), lambda j, i, r: (0, i, 0)))
        out_shape.append(jax.ShapeDtypeStruct((6, rows, total), jnp.bfloat16))
    result = pl.pallas_call(
        body,
        grid_spec=pltpu.PrefetchScalarGridSpec(
            num_scalar_prefetch=1,
            grid=(columns // nb, rows // mb),
            in_specs=in_specs,
            out_specs=out_specs,
            scratch_shapes=scratch,
        ),
        out_shape=out_shape,
        compiler_params=pltpu.CompilerParams(vmem_limit_bytes=58 * 2**20),
        cost_estimate=pl.CostEstimate(flops=1000, bytes_accessed=1000, transcendentals=0),
    )(role, *args)
    return tuple(result) if len(result) > 1 else result[0]


def place_kernel(role_ref, *refs):
    blocks, out = refs[: 4 + CHUNKS], refs[-1]
    for role, sources in ((0, blocks[:1]), (1, blocks[1:4])):

        @pl.when(role_ref[0] == role)
        def _():
            if sources[-1].shape[0] == 2:
                out[:, 0] = sources[0][...]
            else:
                out[0, 0], out[1, 0] = sources[1][0], sources[2][0]

    for step, ref in enumerate(blocks[4:]):

        @pl.when((role_ref[0] >= 2) & (pl.program_id(0) == step))
        def _():
            out[:, 0] = ref[...]


def place(role, first, second, chunks, other, onto=None):
    _, rows, columns = first.shape
    w, steps = columns // CHUNKS, 2
    block = rows // steps
    second = [second] * 3 if not isinstance(second, list) else [second[0]] + second

    def wide(role_, count):
        def at(j, i, r):
            used = jnp.where(r[0] == role_, 1, 0)
            return (0, i * used, j * used)

        return pl.BlockSpec((count, block, w), at)

    def narrow(step):
        return pl.BlockSpec((2, block, w), lambda j, i, r: (0, i * jnp.where((r[0] >= 2) & (j == step), 1, 0), 0))

    def to(j, i, r):
        f = 1 - r[1] if other else r[1]
        return (0, f, i, (j + 2 * f) % CHUNKS)

    in_specs = [wide(0, 2)] + [wide(1, v.shape[0]) for v in second] + [narrow(step) for step in range(CHUNKS)]
    args = [role, first, *second, *chunks]
    if other:
        in_specs.append(pl.BlockSpec(memory_space=pl.ANY))
        args.append(onto)
    return pl.pallas_call(
        place_kernel,
        grid_spec=pltpu.PrefetchScalarGridSpec(
            num_scalar_prefetch=1,
            grid=(CHUNKS, steps),
            in_specs=in_specs,
            out_specs=pl.BlockSpec((2, 1, block, w), to),
        ),
        out_shape=jax.ShapeDtypeStruct((2, 2, rows, columns), jnp.float32),
        input_output_aliases={len(args) - 1: 0} if other else {},
        compiler_params=pltpu.CompilerParams(vmem_limit_bytes=40 * 2**20),
        cost_estimate=pl.CostEstimate(flops=1000, bytes_accessed=1000, transcendentals=0),
    )(*args)


def blocked(recorded):
    row, col = lax.axis_index("row"), lax.axis_index("col")
    z, x, y, c = row // 2, row % 2, col // 2, col % 2
    half, p = z // 2, z % 2
    diag, first, lane = y == half, c == p, c == half
    at_end = (z == 0) | (z == 3)
    role = jnp.where(diag, jnp.where(first, 0, 1), jnp.where(lane, 3, 2) + jnp.where(at_end, 0, 2)).astype(jnp.int32)
    roles = jnp.reshape(role, (1,))
    part, width = recorded.shape[2], recorded.shape[3]
    w, n = width // CHUNKS, width

    def send(value, *moves):
        pairs = []
        for zz in range(4):
            for xx in range(2):
                for yy in range(2):
                    for cc in range(2):
                        for move in moves:
                            to = move(zz, xx, yy, cc)
                            if to is not None:
                                a, b, d, e = to
                                pairs.append((((zz * 2 + xx) * 2 + yy) * 2 + cc, ((a * 2 + b) * 2 + d) * 2 + e))
        return lax.ppermute(value, AXES, pairs)

    def on_diag(zz, yy):
        return yy == zz // 2

    swap_x = lambda a, b, d, e: (a, 1 - b, d, e)
    swap_y = lambda a, b, d, e: (a, b, 1 - d, e)
    swap_core = lambda a, b, d, e: (a, b, d, 1 - e)
    swap_core_diag = lambda a, b, d, e: (a, b, d, 1 - e) if on_diag(a, d) else None
    to_diag = lambda a, b, d, e: None if on_diag(a, d) else (a, b, 1 - d, e)
    to_off = lambda a, b, d, e: (a, b, 1 - d, e) if on_diag(a, d) else None
    swap_slab = lambda a, b, d, e: (a ^ 1, b, d, e) if on_diag(a, d) else None
    first_to_slab = lambda a, b, d, e: (a ^ 1, b, d, e) if on_diag(a, d) and e == a % 2 else None
    over_middle = lambda a, b, d, e: (3 - a, b, d, e) if on_diag(a, d) and a in (1, 2) else None
    middle_second = lambda a, b, d, e: (3 - a, b, d, e) if on_diag(a, d) and a in (1, 2) and e != a % 2 else None
    outward = lambda a, b, d, e: {1: (0, b, d, e), 2: (3, b, d, e)}.get(a) if not on_diag(a, d) else None
    outward_second = lambda a, b, d, e: outward(a, b, d, e) if e != a // 2 else None
    x_first = lambda a, b, d, e: (a, 1 - b, d, e) if on_diag(a, d) and e == a % 2 else None
    x_second = lambda a, b, d, e: (a, 1 - b, d, e) if on_diag(a, d) and e != a % 2 else None
    x_off = lambda a, b, d, e: None if on_diag(a, d) else (a, 1 - b, d, e)

    pick = jnp.where
    sync = lambda *values: lax.optimization_barrier(values)
    mid_off = jnp.logical_not(diag | at_end)

    def cut(f, j):
        start = (j * w + f * part) % width
        return lax.dynamic_slice(recorded, (0, f, 0, start), (2, 1, part, 2 * w))[:, 0]

    def chunk(value, j):
        return value[:, :, j * w : (j + 1) * w]

    mine, give = [cut(x, 0), cut(x, 2)], [cut(1 - x, 0), cut(1 - x, 2)]
    got = send(give[0], swap_x)
    own01 = jnp.concatenate([mine[0], got], 1)
    own = [chunk(own01, 0), chunk(own01, 1)]
    lows = jnp.concatenate([own[0], own[1][:, w:]], 1)
    own01, own[0], own[1], lows, give[1] = sync(own01, own[0], own[1], lows, give[1])

    right, there, seen, cores, seen_cores = [None] * 4, [None] * 4, [None] * 4, [None] * 4, [None] * 4
    got = send(give[1], swap_x)
    right[0] = send(own[0], to_diag, over_middle)
    low01 = send(lows, first_to_slab)
    core01 = send(own01, swap_core)
    own23 = jnp.concatenate([mine[1], got], 1)
    own += [chunk(own23, 0), chunk(own23, 1)]
    lows23 = jnp.concatenate([own[2][:, 2 * w :], own[3][:, 3 * w :]], 1)
    mixed = pick(diag & first, jnp.concatenate([own[1][:, w:], own[3][:, 3 * w :]], 1), own[1])
    own23, own[2], own[3], lows23, mixed, right[0], low01, core01 = sync(
        own23, own[2], own[3], lows23, mixed, right[0], low01, core01
    )
    core23 = send(own23, swap_core)

    def whole(which, k, row, transposed=False):
        return (which, 0, k, transposed, row, 0)

    def lower(sources, j, row, col):
        out = [(sources[i][0], sources[i][1] + (j - i) * w, w, True, row + i * w, col) for i in range(j)]
        return out + [(sources[j][0], sources[j][1], n - j * w, False, row + j * w, col)]

    there[0] = send(right[0], swap_slab, outward)
    right[1] = send(mixed, to_diag, over_middle)
    low23 = send(lows23, first_to_slab)
    cores[0] = send(right[0], swap_core_diag)
    both = [whole(0, n, 0, True), whole(1, n, n // 2, True)]
    total, left = product(
        roles,
        [own01, own23, core01, core23],
        [core01, core23, own01, own23],
        {0: [both], 1: [[whole(2, n, 0), (3, 0, n, False, 0, n // 2)]]},
        n,
        fetch=True,
        keep=True,
    )
    there[0], right[1], total, left = sync(there[0], right[1], total, left)
    there[1] = send(right[1], swap_slab, outward)
    mixed = pick(diag & first, chunk(core23, 1), own[2])
    seen[0] = pick(mid_off, right[0], there[0])
    there[0], right[1], low01, low23, cores[0], left, total, mixed, seen[0], own[3] = sync(
        there[0], right[1], low01, low23, cores[0], left, total, mixed, seen[0], own[3]
    )

    def share(j):
        r, t = right[j], there[j]
        return product(
            roles, left, [r, t], {0: [[whole(0, n, 0), whole(1, n, n)]], 1: [[whole(1, n, 0), whole(0, n, n)]]}, w
        )

    def add_rights(total, js, active, halves=1):
        these = [right[j] for j in js] + [cores[j] for j in js]
        others = [there[j] for j in js] + [seen_cores[j] for j in js]
        k = len(these)
        rights = (these if 0 in active else []) + (others if 1 in active else [])
        first_of = {0: 0, 1: len(rights) - k}
        picks = {v: [[(first_of[v] + i, 0, n, False, 0, i * w) for i in range(k)]] for v in active}
        return product(roles, these, rights, picks, n, base=total, halves=halves, fetch=True, negate=halves > 1, by_rows=True)

    shares, shared = [None] * 4, [None] * 4
    right[2] = send(mixed, to_diag, over_middle)
    cores[1] = send(right[1], swap_core_diag)
    seen_cores[0] = send(seen[0], swap_core)
    shares[0] = share(0)
    low_sources = [(2, 0), (2, n), (3, 0), (3, 2 * w)]
    total = product(
        roles,
        left,
        [own01, own23, low01, low23],
        {
            0: [[(0, 0, n, False, 0, 0), (1, 0, n, False, 0, n // 2)]],
            1: [sum([lower(low_sources, j, 0, j * w) for j in range(4)], [])],
        },
        n,
        base=total,
        half=0,
        fetch=True,
        by_rows=True,
    )
    right[2], total = sync(right[2], total)
    there[2] = send(right[2], swap_slab, outward)
    mixed = pick(diag, shares[0], own[3])
    seen[1] = pick(mid_off, right[1], there[1])
    there[1], right[2], low01, low23, cores[1], seen_cores[0], total, mixed, seen[1] = sync(
        there[1], right[2], low01, low23, cores[1], seen_cores[0], total, mixed, seen[1]
    )

    right[3] = send(mixed, swap_y)
    near3 = send(low01, middle_second)
    cores[2] = send(right[2], swap_core_diag)
    seen_cores[1] = send(seen[1], swap_core)
    shares[1] = share(1)
    shares[1], seen_cores[1], cores[1], total = sync(shares[1], seen_cores[1], cores[1], total)
    total = add_rights(total, (0, 1), (0, 1))
    right[3], total = sync(right[3], total)
    there[3] = send(right[3], swap_slab)
    mixed = pick(diag & first, lows23, low23)
    swapped = pick(diag, right[3], pick(mid_off, right[2], there[2]))
    there[2], right[3], near3, cores[2], shares[1], total, swapped, mixed = sync(
        there[2], right[3], near3, cores[2], shares[1], total, swapped, mixed
    )
    shared[0] = right[3]

    shared[1] = send(shares[1], to_off)
    near4 = send(mixed, over_middle)
    far3 = send(near3, outward_second)
    swapped = send(swapped, swap_core)
    shares[2] = share(2)
    shares[2], total, swapped = sync(shares[2], total, swapped)
    cores[3] = swapped
    keep_first, to_first = add_rights(total, (2, 3), (0,), 2)
    to_first, swapped, far3, near3 = sync(to_first, swapped, far3, near3)

    far4 = near4

    def rest(j, base):
        rights = seen[:2] + [there[2]] + seen_cores[:2] + [swapped, far3, far4, near3, near4, right[2]]
        picks = {}
        for k, last, third in ((2, 6, 2), (4, 8, 10)):
            lane_low = [(0, 0), (1, 0), (last + 1, 0), (1, 3 * w)]
            other_low = [(last, 0), (last, n), (last + 1, 0), (last + 1, 2 * w)]
            picks[k] = lower(other_low, j, 0, 0) + [whole((0, 1, third, 5)[j], n, n)]
            picks[k + 1] = lower(lane_low, j, 0, 0)
            picks[k + 1] += [(v, j * w, w, True, n + i * w, 0) for i, v in enumerate((3, 4, 5, third))]
        used = sorted({entry[0] for pieces in picks.values() for entry in pieces})
        picks = {r: [[(used.index(e[0]),) + e[1:] for e in v]] for r, v in picks.items()}
        return product(roles, left, [rights[i] for i in used], picks, w, base=base, halves=2, fetch=True, negate=True)

    tops, downs, crossed = [None] * 4, [None] * 4, [None] * 4
    tops[0], downs[0] = rest(0, shared[0])
    there[3], shared[1], near4, far3, swapped, shares[2], keep_first, to_first, total, downs[0] = sync(
        there[3], shared[1], near4, far3, swapped, shares[2], keep_first, to_first, total, downs[0]
    )

    far4 = send(near4, outward)
    shared[2] = send(shares[2], to_off)
    seen_cores[2] = send(there[2], swap_core_diag)
    got_first = send(to_first, x_first)
    seen_cores[3] = send(there[3], swap_core_diag)
    crossed[0] = send(downs[0], x_off)
    shares[3] = share(3)
    shares[3], shared[1], seen_cores[2], seen_cores[3] = sync(shares[3], shared[1], seen_cores[2], seen_cores[3])
    shared[3] = send(shares[3], to_off)
    tops[1], downs[1] = rest(1, shared[1])
    downs[1], total, crossed[0] = sync(downs[1], total, crossed[0])
    crossed[1] = send(downs[1], x_off)
    keep_second, *to_second = add_rights(total, (2, 3), (1,), 3)
    to_second[0], to_second[1], shared[2], far4 = sync(*to_second, shared[2], far4)
    got_second = [send(v, x_second) for v in to_second]
    tops[2], downs[2] = rest(2, shared[2])
    downs[2], crossed[1], got_first, far3 = sync(downs[2], crossed[1], got_first, far3)
    crossed[2] = send(downs[2], x_off)
    tops[3], downs[3] = rest(3, None)
    tops[3], downs[3], shared[3], crossed[2] = sync(tops[3], downs[3], shared[3], crossed[2])
    downs[3] = downs[3] - shared[3][:, part:]
    crossed[3] = send(downs[3], x_off)
    tops[3] = tops[3] - shared[3][:, :part]

    flags = jnp.stack([role, x.astype(jnp.int32)])
    out = place(flags, keep_first, keep_second, tops, False)
    return place(flags, got_first, got_second, crossed, True, out)


def solution(mesh):
    rows, cols = mesh.shape["row"], mesh.shape["col"]

    def body(recorded):
        frequencies = recorded.shape[1]
        if frequencies == 2 and cols == 4 and rows == frequencies * cols:
            return blocked(recorded)
        return gathered(recorded)

    spec = P(None, None, "row", "col")
    return jax.shard_map(body, mesh=mesh, in_specs=(spec,), out_specs=spec, check_vma=False)
```
